32 devices in a mesh: groups: 2 (over x), img: 16 (over z, y, core).
Axes of the slice: x: 2, y: 2, z: 4, core: 2. Of those that a mesh axis runs over, the one named last changes fastest.
Arguments:
- tokens: bfloat16 [64, 128, 768], P(('groups', 'img')), parts along dimension 0, may hold values from -6 to 6
- partners: int32 [64, 8], P(('groups', 'img')), parts along dimension 0, may hold values from 0 to 31, as said below
- counts: int32 [64], P(('groups', 'img')), parts along dimension 0, may hold values from 4 to 8, as said below
- gain_query: float32 [768], replicated, may hold values from 0.5 to 12
- gain_memory: float32 [768], replicated, may hold values from 0.25 to 1.75
- w_query: bfloat16 [768, 768], replicated, may hold values from -0.21875 to 0.21875
- w_key: bfloat16 [768, 768], replicated, may hold values from -0.21875 to 0.21875
- w_value: bfloat16 [768, 768], replicated, may hold values from -0.21875 to 0.21875
- w_out: bfloat16 [768, 768], replicated, may hold values from -0.21875 to 0.21875
Outputs:
- mixed: bfloat16 [64, 128, 768], P(('groups', 'img')), parts along dimension 0
The draws below stay inside these ranges and needn't reach their ends.
There are 2 independent parts, one for each index of `groups`. The reference program is written for one: setup_inputs(seed, part) draws one part's arguments, and reference() takes and returns one part's arrays. A program takes and returns all parts, laid end to end along the dimension named above; an argument that names none is the same for every part. Nothing has to cross between parts.
Inputs may be any that keep to these rules, and one draw needn't show every extreme that they name: No image is its own partner. Over the first counts[a] partners of all images a of one device (image i belongs to device i // 2), at most 1 lie with any one device, and every device reaches 1 with some device. `counts`: every device owns an image with 8 pairs.
All inputs are finite; a program needn't handle non-finite values.
Results may differ from the reference program's by a relative error of at most 0.0067.
Values may be sent and summed in bfloat16 or wider, within the bound.
No kernel may reach another device: no remote copies, remote signals or barrier semaphores. Data moves between devices by JAX's collectives and lax.ppermute only.
A program may use at most 128 MiB of HBM per device.

```python
import jax
import jax.numpy as jnp
from jax import lax

D = 768
HEADS = 12
HEAD_DIM = 64
TOK = 128
PARTNERS = 8
IMG_DEV = 2
IMAGES = 32
CAP = 1


def scene_graph(key):
    device_count = IMAGES // IMG_DEV
    pieces = jax.random.split(jax.random.fold_in(key, 7), 6)
    pair_counts = jax.random.randint(pieces[0], (device_count, IMG_DEV), PARTNERS // 2, PARTNERS + 1)
    full_image = jax.random.randint(pieces[2], (device_count,), 0, IMG_DEV)
    pair_counts = jnp.where(jnp.arange(IMG_DEV)[None, :] == full_image[:, None], PARTNERS, pair_counts)
    live = (jnp.arange(PARTNERS)[None, None, :] < pair_counts[:, :, None]).reshape(device_count, IMG_DEV * PARTNERS)
    rank = jnp.cumsum(live.astype(jnp.int32), axis=1) - 1
    orders = jax.vmap(lambda sub: jax.random.permutation(sub, device_count))(jax.random.split(pieces[3], device_count))
    slot_owner = jnp.take_along_axis(orders, jnp.clip(rank // CAP, 0, device_count - 1), axis=1)
    other_owner = jax.random.randint(pieces[4], (device_count, IMG_DEV * PARTNERS), 0, device_count)
    owner = jnp.where(live, slot_owner, other_owner)
    within = jax.random.randint(pieces[5], (device_count, IMG_DEV * PARTNERS), 0, IMG_DEV)
    query_image = jnp.arange(device_count)[:, None] * IMG_DEV + jnp.repeat(jnp.arange(IMG_DEV), PARTNERS)[None, :]
    partner = owner * IMG_DEV + within
    partner = jnp.where(partner == query_image, owner * IMG_DEV + (within + 1) % IMG_DEV, partner)
    return (pair_counts.reshape(IMAGES).astype(jnp.int32), partner.reshape(IMAGES, PARTNERS).astype(jnp.int32))


def draw_partners(key, part):
    return scene_graph(key)[1]


def draw_counts(key, part):
    return scene_graph(key)[0]


def draw_gain_query(key, part):
    gain = jnp.exp(jax.random.uniform(key, (D,), jnp.float32, jnp.log(0.5), jnp.log(2.0)))
    return gain.astype(jnp.float32)


def level_of(own_key, dims, cuts, smallest, largest):
    def one(axis_at, blocks):
        steps = jax.random.uniform(jax.random.fold_in(jax.random.fold_in(own_key, 6), axis_at), (blocks,), jnp.float32, smallest / len(cuts), largest / len(cuts))
        return jnp.repeat(jnp.exp(steps), dims[axis_at] // blocks).reshape((-1,) + (1,) * (len(dims) - axis_at - 1))

    loudness = one(*cuts[0])
    for cut in cuts[1:]:
        loudness = loudness * one(*cut)
    return loudness


def centred(own_key, shape, width, bound, cuts=(), kind=jnp.bfloat16):
    factor_of = level_of(own_key, shape, cuts, -0.22, 0.18) if cuts else 1.0
    drawn = jax.random.normal(own_key, shape, jnp.float32) * width * factor_of
    return jnp.minimum(jnp.maximum(drawn, -bound), bound).astype(kind)


def setup_inputs(seed: int = 0, part: int = 0) -> dict:
    streams_of = jax.random.split(jax.random.key(seed), 10)
    own_keys = jax.random.split(jax.random.fold_in(streams_of[9], part), 10)
    tokens = centred(own_keys[0], (IMAGES, TOK, D), 1.0, 6.0, ((0, 16),))
    partners = draw_partners(jax.random.fold_in(jax.random.fold_in(streams_of[9], part), 71), part)
    counts = draw_counts(jax.random.fold_in(jax.random.fold_in(streams_of[9], part), 71), part)
    gain_query = draw_gain_query(jax.random.fold_in(streams_of[9], 71), part)
    gain_memory = jnp.clip(1.0 + 0.15 * jax.random.normal(streams_of[4], (D,), jnp.float32), 0.25, 1.75)
    w_query = centred(streams_of[5], (D, D), D ** -0.5, 0.21875)
    w_key = centred(streams_of[6], (D, D), D ** -0.5, 0.21875)
    w_value = centred(streams_of[7], (D, D), D ** -0.5, 0.21875)
    w_out = centred(streams_of[8], (D, D), D ** -0.5, 0.21875)
    return dict(tokens=tokens, partners=partners, counts=counts, gain_query=gain_query, gain_memory=gain_memory, w_query=w_query, w_key=w_key, w_value=w_value, w_out=w_out)


def normalize(rows, gain):
    rows = rows.astype(jnp.float32)
    center = rows - lax.optimization_barrier(jnp.mean(rows, axis=-1, keepdims=True))
    spread = lax.optimization_barrier(jnp.mean(center * center, axis=-1, keepdims=True))
    return center * lax.rsqrt(spread + 1e-06) * gain

def reference(tokens, partners, counts, gain_query, gain_memory, w_query, w_key, w_value, w_out):
    rows = tokens.reshape(IMAGES * TOK, D)
    normed_query = normalize(rows, gain_query).astype(jnp.bfloat16)
    normed_memory = normalize(rows, gain_memory).astype(jnp.bfloat16)
    queries = jnp.dot(normed_query, w_query, preferred_element_type=jnp.float32).astype(jnp.bfloat16)
    keys = jnp.dot(normed_memory, w_key, preferred_element_type=jnp.float32).astype(jnp.bfloat16)
    values = jnp.dot(normed_memory, w_value, preferred_element_type=jnp.float32).astype(jnp.bfloat16)
    queries = queries.reshape(IMAGES, TOK, HEADS, HEAD_DIM)
    keys = keys.reshape(IMAGES, TOK, HEADS, HEAD_DIM)
    values = values.reshape(IMAGES, TOK, HEADS, HEAD_DIM)
    scale = 1.0 / math_sqrt(HEAD_DIM)

    def one_image(item):
        query_rows, partner_row, count = item
        key_rows = keys[partner_row.astype(jnp.int32)].astype(jnp.float32)
        value_rows = values[partner_row.astype(jnp.int32)].astype(jnp.float32)
        scores = jnp.einsum('qhd,kjhd->hkqj', query_rows.astype(jnp.float32), key_rows) * scale
        probs = lax.optimization_barrier(jax.nn.softmax(scores, axis=-1).astype(jnp.bfloat16)).astype(jnp.float32)
        pair_context = jnp.einsum('hkqj,kjhd->kqhd', probs, value_rows)
        live = jnp.arange(PARTNERS, dtype=jnp.int32) < count
        total = lax.optimization_barrier(jnp.sum(jnp.where(live[:, None, None, None], pair_context, jnp.float32(0.0)), axis=0))
        return total.reshape(TOK, D) / count.astype(jnp.float32)
    context = lax.map(one_image, (queries, partners, counts)).astype(jnp.bfloat16)
    mixed = rows.astype(jnp.float32) + jnp.dot(context.reshape(IMAGES * TOK, D), w_out, preferred_element_type=jnp.float32)
    return mixed.astype(jnp.bfloat16).reshape(IMAGES, TOK, D)

def math_sqrt(value):
    return value ** 0.5
```

```python
import functools

import jax
import jax.numpy as jnp
from jax import lax
from jax.experimental import pallas as pl
from jax.experimental.pallas import tpu as pltpu
from jax.sharding import PartitionSpec as P

HEADS = 12
HEAD_DIM = 64
CORES = 2
PAIRED = 2 * HEAD_DIM


class Ring:
    def __init__(self, devices, columns):
        self.chips = devices // CORES
        self.columns = columns
        self.rows = self.chips // columns

    def chip(self, place):
        if self.columns == 1:
            return place
        if place < self.rows:
            return place * 2
        return (2 * self.rows - 1 - place) * 2 + 1

    def onward(self):
        pairs = []
        for place in range(self.chips):
            for core, step in ((0, 1), (1, -1)):
                target = self.chip((place + step) % self.chips)
                pairs.append((self.chip(place) * CORES + core, target * CORES + core))
        return pairs

    def sibling(self):
        return [(i, i ^ 1) for i in range(self.chips * CORES)]

    def owner(self, me, step, flip):
        chip = me // CORES
        core = lax.rem(me, CORES)
        if self.columns == 1:
            place = chip
        else:
            row = chip // 2
            place = jnp.where(lax.rem(chip, 2) == 0, row, 2 * self.rows - 1 - row)
        if flip:
            core = 1 - core
        came = lax.rem(place + self.chips + jnp.where(core == 0, -step, step), self.chips)
        if self.columns == 1:
            there = came
        else:
            there = jnp.where(came < self.rows, came * 2, (2 * self.rows - 1 - came) * 2 + 1)
        return there * CORES + core


def normalize(rows, gain):
    rows = rows.astype(jnp.float32)
    center = rows - jnp.mean(rows, axis=-1, keepdims=True)
    spread = jnp.mean(center * center, axis=-1, keepdims=True)
    return center * lax.rsqrt(spread + 1e-06) * gain


def dot(a, b, dims=((1,), (0,))):
    return lax.dot_general(a, b, (dims, ((), ())), preferred_element_type=jnp.float32)


def find_slot(owner, partners, counts, own, listed):
    image = jnp.int32(0)
    index = jnp.int32(0)
    live = jnp.int32(0)
    for a in range(own):
        for k in range(listed):
            partner = partners[a, k]
            hit = jnp.logical_and(k < counts[a], partner // own == owner)
            image = jnp.where(hit, a, image)
            index = jnp.where(hit, lax.rem(partner, own), index)
            live = jnp.where(hit, 1, live)
    return image, index, live


def stage_kernel(ring, slots, first, last, own, listed, tok, *refs):
    refs = list(refs)
    take = lambda n: [refs.pop(0) for _ in range(n)]
    sources = [take(own) for _ in slots]
    partners, counts, gain_memory, w_key = take(4)
    if first:
        tokens, gain_query, w_query, w_value = take(4)
    else:
        w_value_t, spread_q, total_in = take(3)
    if last:
        tokens, w_out = take(2)
    if last:
        (mixed,) = take(1)
        total = refs.pop()
    elif first:
        total, spread_q, w_value_t = take(3)
    else:
        (total,) = take(1)
    memory, sems = take(2)

    me = lax.axis_index("img")
    found = [find_slot(ring.owner(me, step, flip), partners, counts, own, listed) for step, flip in slots]
    for at, (image, index, live) in enumerate(found):
        for j in range(own):

            @pl.when(index == j)
            def _():
                pltpu.make_async_copy(sources[at][j], memory.at[at], sems.at[at]).start()

    if first:
        rows = tokens[...].reshape(own * tok, -1)
        normed_query = normalize(rows, gain_query[...]).astype(jnp.bfloat16)
        queries = dot(normed_query, w_query[...]).astype(jnp.bfloat16).astype(jnp.float32)
        queries_t = (queries * (1.0 / HEAD_DIM**0.5)).T.astype(jnp.bfloat16)
        zero = jnp.zeros((HEAD_DIM, tok), jnp.bfloat16)
        for a in range(own):
            for h in range(HEADS):
                part = queries_t[h * HEAD_DIM : (h + 1) * HEAD_DIM, a * tok : (a + 1) * tok]
                pieces = [part, zero] if h % 2 == 0 else [zero, part]
                spread_q[a, h * HEAD_DIM : (h + 1) * HEAD_DIM, :] = jnp.concatenate(pieces, axis=1)
        w_value_t[...] = w_value[...].astype(jnp.float32).T.astype(jnp.bfloat16)
        total[...] = jnp.zeros_like(total)
    else:
        total[...] = total_in[...]

    for at in range(len(slots)):
        pltpu.make_async_copy(sources[at][0], memory.at[at], sems.at[at]).wait()
    rows = memory[...].reshape(len(slots) * tok, -1)
    normed = normalize(rows, gain_memory[...]).astype(jnp.bfloat16)
    keys = dot(normed, w_key[...]).astype(jnp.bfloat16)
    values_t = dot(w_value_t[...], normed, ((1,), (1,))).astype(jnp.bfloat16)
    for at, (image, index, live) in enumerate(found):
        here = slice(at * tok, (at + 1) * tok)
        for g in range(HEADS // 2):
            both = slice(g * PAIRED, (g + 1) * PAIRED)
            scores = dot(keys[here, both], spread_q[image, both, :])
            weights = jnp.exp(scores - jnp.max(scores, axis=0, keepdims=True))
            share = live.astype(jnp.float32) / jnp.sum(weights, axis=0, keepdims=True)
            weights = weights.astype(jnp.bfloat16)
            for h in range(2):
                feats = slice(g * PAIRED + h * HEAD_DIM, g * PAIRED + (h + 1) * HEAD_DIM)
                asked = slice(h * tok, (h + 1) * tok)
                part = dot(values_t[feats, here], weights[:, asked])
                total[image, feats, :] += part * share[:, asked]

    if last:
        for a in range(own):
            context = (total[a] / counts[a].astype(jnp.float32)).T.astype(jnp.bfloat16)
            out = tokens[a].astype(jnp.float32) + dot(context, w_out[...])
            mixed[a] = out.astype(jnp.bfloat16)


def stage(ring, slots, sources, shared, extra, first, last, own, listed, tok, width):
    smem = pl.BlockSpec(memory_space=pltpu.SMEM)
    vmem = pl.BlockSpec(memory_space=pltpu.VMEM)
    where = [pl.BlockSpec(memory_space=pl.ANY)] * (len(slots) * own) + [smem, smem]
    where += [vmem] * (2 + len(extra))
    operands = [image for images in sources for image in images] + list(shared) + list(extra)
    total = jax.ShapeDtypeStruct((own, width, tok), jnp.float32)
    spread_q = jax.ShapeDtypeStruct((own, width, 2 * tok), jnp.bfloat16)
    w_value_t = jax.ShapeDtypeStruct((width, width), jnp.bfloat16)
    scratch = [pltpu.VMEM((len(slots), tok, width), jnp.bfloat16), pltpu.SemaphoreType.DMA((len(slots),))]
    aliases = {}
    if last:
        shapes = [jax.ShapeDtypeStruct((own, tok, width), jnp.bfloat16)]
        scratch.append(pltpu.VMEM(total.shape, total.dtype))
    elif first:
        shapes = [total, spread_q, w_value_t]
    else:
        shapes = [total]
        aliases = {len(slots) * own + 6: 0}
    rows = len(slots) * tok
    return pl.pallas_call(
        functools.partial(stage_kernel, ring, slots, first, last, own, listed, tok),
        out_shape=shapes,
        in_specs=where,
        out_specs=[vmem] * len(shapes),
        scratch_shapes=scratch,
        input_output_aliases=aliases,
        compiler_params=pltpu.CompilerParams(vmem_limit_bytes=32 << 20),
        cost_estimate=pl.CostEstimate(
            flops=4 * rows * width * (width + tok) * 2,
            bytes_accessed=2 * width * width * 2 + 3 * rows * width * 2,
            transcendentals=rows * tok * HEADS,
        ),
    )(*operands)


def shards(columns, tokens, partners, counts, gain_query, gain_memory, w_query, w_key, w_value, w_out):
    own, tok, width = tokens.shape
    listed = partners.shape[1]
    ring = Ring(lax.axis_size("img"), columns)
    onward, sibling = ring.onward(), ring.sibling()
    gain_query = gain_query.reshape(1, width)
    gain_memory = gain_memory.reshape(1, width)
    shared = (partners, counts, gain_memory, w_key)
    call = functools.partial(stage, ring, own=own, listed=listed, tok=tok, width=width)

    mine = [tokens[j] for j in range(own)]
    theirs = [lax.ppermute(image, "img", sibling) for image in mine]
    for step in range(ring.chips):
        first, last = step == 0, step == ring.chips - 1
        slots = ((step, False), (step, True))
        if first:
            extra = (tokens, gain_query, w_query, w_value)
        else:
            extra = (w_value_t, spread_q, total)
        if last:
            extra += (tokens, w_out)
        if not last:
            mine_next = [lax.ppermute(image, "img", onward) for image in mine]
            theirs_next = [lax.ppermute(image, "img", sibling) for image in mine_next]
        out = call(slots, (mine, theirs), shared, extra, first, last)
        if last:
            return out[0]
        if first:
            total, spread_q, w_value_t = out
        else:
            (total,) = out
        mine, theirs = mine_next, theirs_next


def solution(mesh):
    placed = (
        P(("groups", "img"), None, None),
        P(("groups", "img"), None),
        P(("groups", "img")),
        P(),
        P(),
        P(),
        P(),
        P(),
        P(),
    )
    columns = max(1, 4 // mesh.shape["groups"])
    return jax.shard_map(
        functools.partial(shards, columns),
        mesh=mesh,
        in_specs=placed,
        out_specs=P(("groups", "img"), None, None),
        check_vma=False,
    )
```

```python
import functools

import jax
import jax.numpy as jnp
from jax import lax
from jax.experimental import pallas as pl
from jax.experimental.pallas import tpu as pltpu
from jax.sharding import PartitionSpec as P

HEADS = 12
HEAD_DIM = 64
CORES = 2
PAIRED = 2 * HEAD_DIM


class Ring:
    def __init__(self, devices, columns):
        self.chips = devices // CORES
        self.columns = columns
        self.rows = self.chips // columns

    def chip(self, place):
        if self.columns == 1:
            return place
        if place < self.rows:
            return place * 2
        return (2 * self.rows - 1 - place) * 2 + 1

    def onward(self, step):
        pairs = []
        for place in range(self.chips):
            target = self.chip((place + step) % self.chips)
            pairs += [(self.chip(place) * CORES + core, target * CORES + core) for core in range(CORES)]
        return pairs

    def sibling(self):
        return [(i, i ^ 1) for i in range(self.chips * CORES)]

    def owner(self, me, shift, flip):
        chip = me // CORES
        core = lax.rem(me, CORES)
        if flip:
            core = 1 - core
        if self.columns == 1:
            place = chip
        else:
            row = chip // 2
            place = jnp.where(lax.rem(chip, 2) == 0, row, 2 * self.rows - 1 - row)
        came = lax.rem(place + shift + self.chips, self.chips)
        if self.columns == 1:
            there = came
        else:
            there = jnp.where(came < self.rows, came * 2, (2 * self.rows - 1 - came) * 2 + 1)
        return there * CORES + core


def normalize(rows, gain):
    rows = rows.astype(jnp.float32)
    center = rows - jnp.mean(rows, axis=-1, keepdims=True)
    spread = jnp.mean(center * center, axis=-1, keepdims=True)
    return center * lax.rsqrt(spread + 1e-06) * gain


def dot(a, b, dims=((1,), (0,))):
    return lax.dot_general(a, b, (dims, ((), ())), preferred_element_type=jnp.float32)


def find_slot(owner, partners, counts, own, listed):
    image = jnp.int32(0)
    index = jnp.int32(0)
    live = jnp.int32(0)
    for a in range(own):
        for k in range(listed):
            partner = partners[a, k]
            hit = jnp.logical_and(k < counts[a], partner // own == owner)
            image = jnp.where(hit, a, image)
            index = jnp.where(hit, lax.rem(partner, own), index)
            live = jnp.where(hit, 1, live)
    return image, index, live


def attend(memory, slots, gain, w_kv, spread_q, total, tok):
    width = memory.shape[-1]
    normed = normalize(memory, gain).astype(jnp.bfloat16)
    both = dot(normed, w_kv[...]).astype(jnp.bfloat16)
    for at, (image, live) in enumerate(slots):
        here = slice(at * tok, (at + 1) * tok)
        for g in range(HEADS // 2):
            feats = slice(g * PAIRED, (g + 1) * PAIRED)
            scores = dot(both[here, feats], spread_q[image, feats, :])
            weights = jnp.exp(scores - jnp.max(scores, axis=0, keepdims=True))
            share = live.astype(jnp.float32) / jnp.sum(weights, axis=0, keepdims=True)
            weights = weights.astype(jnp.bfloat16)
            parts = []
            for h in range(2):
                values = both[here, width + g * PAIRED + h * HEAD_DIM : width + g * PAIRED + (h + 1) * HEAD_DIM]
                asked = slice(h * tok, (h + 1) * tok)
                parts.append(dot(values, weights[:, asked], ((0,), (0,))) * share[:, asked])
            total[image, feats, :] += jnp.concatenate(parts, axis=0)


def first_kernel(ring, slots, own, listed, tok, *refs):
    (tokens, partners, counts, gain_query, gain_memory, w_query, w_key, w_value, w_out) = refs[:9]
    total, spread_q, w_kv, w_out_here, tokens_here, gain_here, picks, table = refs[9:17]
    partners_here, counts_here, gain_query_here, w_query_here, sems = refs[17:]
    width = tokens.shape[-1]
    copies = [
        pltpu.make_async_copy(source, target, sems.at[i])
        for i, (source, target) in enumerate(
            (
                (partners, partners_here),
                (counts, counts_here),
                (tokens, tokens_here),
                (gain_query, gain_query_here),
                (w_query, w_query_here),
                (gain_memory, gain_here),
                (w_key, w_kv.at[:, pl.ds(0, width)]),
                (w_value, w_kv.at[:, pl.ds(width, width)]),
                (w_out, w_out_here),
            )
        )
    ]
    for copy in copies:
        copy.start()
    total[...] = jnp.zeros_like(total)
    for copy in copies[:2]:
        copy.wait()
    for owner in range(ring.chips * CORES):
        image, index, live = find_slot(owner, partners_here, counts_here, own, listed)
        table[0, owner] = image
        table[1, owner] = live
        picks[owner] = jnp.full(picks.shape[1:], index.astype(jnp.float32))
    for copy in copies[2:5]:
        copy.wait()
    rows = tokens_here[...].reshape(own * tok, -1)
    normed_query = normalize(rows, gain_query_here[...][None, :]).astype(jnp.bfloat16)
    queries = dot(normed_query, w_query_here[...]).astype(jnp.bfloat16).astype(jnp.float32)
    queries_t = (queries * (1.0 / HEAD_DIM**0.5)).T.astype(jnp.bfloat16)
    zero = jnp.zeros((HEAD_DIM, tok), jnp.bfloat16)
    for a in range(own):
        for h in range(HEADS):
            part = queries_t[h * HEAD_DIM : (h + 1) * HEAD_DIM, a * tok : (a + 1) * tok]
            pieces = [part, zero] if h % 2 == 0 else [zero, part]
            spread_q[a, h * HEAD_DIM : (h + 1) * HEAD_DIM, :] = jnp.concatenate(pieces, axis=1)
    for copy in copies[5:8]:
        copy.wait()
    me = lax.axis_index("img")
    chosen, asked = [], []
    for shift, flip, _ in slots:
        owner = ring.owner(me, shift, flip)
        chosen.append(choose([tokens_here[j] for j in range(own)], picks[owner][:1, :]))
        asked.append((table[0, owner], table[1, owner]))
    attend(jnp.concatenate(chosen, axis=0), asked, gain_here[...][None, :], w_kv, spread_q, total, tok)
    copies[8].wait()


def choose(images, pick):
    chosen = images[0].astype(jnp.float32)
    for j in range(1, len(images)):
        chosen = jnp.where(pick == j, images[j].astype(jnp.float32), chosen)
    return chosen


def later_kernel(ring, slots, last, own, tok, *refs):
    refs = list(refs)
    take = lambda n: [refs.pop(0) for _ in range(n)]
    sources = [take(n) for _, _, n in slots]
    spread_q, w_kv, gain, picks, table, _ = take(6)
    if last:
        w_out, tokens, counts, total, mixed, counts_here, table_here, sems = refs
    else:
        total, table_here, sems = refs
    copies = [pltpu.make_async_copy(table, table_here, sems.at[0])]
    if last:
        copies.append(pltpu.make_async_copy(counts, counts_here, sems.at[1]))
    for copy in copies:
        copy.start()
    me = lax.axis_index("img")
    owners = [ring.owner(me, shift, flip) for shift, flip, _ in slots]
    chosen = []
    for arrays, owner in zip(sources, owners):
        images = [arrays[0][j] for j in range(own)] if len(arrays) == 1 else [array[...] for array in arrays]
        chosen.append(choose(images, picks[owner][:1, :]))
    for copy in copies:
        copy.wait()
    asked = [(table_here[0, owner], table_here[1, owner]) for owner in owners]
    attend(jnp.concatenate(chosen, axis=0), asked, gain[...][None, :], w_kv, spread_q, total, tok)
    if last:
        for a in range(own):
            context = (total[a] / counts_here[a].astype(jnp.float32)).T.astype(jnp.bfloat16)
            out = tokens[a].astype(jnp.float32) + dot(context, w_out[...])
            mixed[a] = out.astype(jnp.bfloat16)


HBM = pl.BlockSpec(memory_space=pltpu.HBM)
ANY = pl.BlockSpec(memory_space=pl.ANY)
SMEM = pl.BlockSpec(memory_space=pltpu.SMEM)
VMEM = pl.BlockSpec(memory_space=pltpu.VMEM)


def cost(rows, tok, width):
    return pl.CostEstimate(
        flops=4 * rows * width * (width + tok) * 2,
        bytes_accessed=2 * width * width * 2 + 3 * rows * width * 2,
        transcendentals=rows * tok * HEADS,
    )


def first_stage(ring, slots, operands, own, listed, tok, width):
    devices = ring.chips * CORES
    shapes = [
        jax.ShapeDtypeStruct((own, width, tok), jnp.float32),
        jax.ShapeDtypeStruct((own, width, 2 * tok), jnp.bfloat16),
        jax.ShapeDtypeStruct((width, 2 * width), jnp.bfloat16),
        jax.ShapeDtypeStruct((width, width), jnp.bfloat16),
        jax.ShapeDtypeStruct((own, tok, width), jnp.bfloat16),
        jax.ShapeDtypeStruct((width,), jnp.float32),
        jax.ShapeDtypeStruct((devices, 8, width), jnp.float32),
        jax.ShapeDtypeStruct((2, devices), jnp.int32),
    ]
    return pl.pallas_call(
        functools.partial(first_kernel, ring, slots, own, listed, tok),
        out_shape=shapes,
        in_specs=[HBM] * len(operands),
        out_specs=[VMEM] * 7 + [SMEM],
        scratch_shapes=[
            pltpu.SMEM((own, listed), jnp.int32),
            pltpu.SMEM((own,), jnp.int32),
            pltpu.VMEM((width,), jnp.float32),
            pltpu.VMEM((width, width), jnp.bfloat16),
            pltpu.SemaphoreType.DMA((9,)),
        ],
        compiler_params=pltpu.CompilerParams(vmem_limit_bytes=32 << 20),
        cost_estimate=cost(own * tok, tok, width),
    )(*operands)


def later_stage(ring, work, state, extra, total, own, tok, width):
    slots, sources = zip(*work)
    last = len(extra) > 0
    images = [array for arrays in sources for array in arrays]
    shapes = [jax.ShapeDtypeStruct(total.shape, total.dtype)]
    scratch = [pltpu.SMEM((2, ring.chips * CORES), jnp.int32), pltpu.SemaphoreType.DMA((2,))]
    if last:
        shapes.append(jax.ShapeDtypeStruct((own, tok, width), jnp.bfloat16))
        scratch = [pltpu.SMEM((own,), jnp.int32)] + scratch
    return pl.pallas_call(
        functools.partial(later_kernel, ring, slots, last, own, tok),
        out_shape=shapes,
        in_specs=[VMEM] * (len(images) + 4) + [ANY, VMEM] + ([VMEM, VMEM, ANY] if last else []),
        out_specs=[VMEM] * len(shapes),
        scratch_shapes=scratch,
        input_output_aliases={len(images) + 5: 0},
        compiler_params=pltpu.CompilerParams(vmem_limit_bytes=32 << 20),
        cost_estimate=cost(len(slots) * tok, tok, width),
    )(*images, *state, total, *extra)


def shards(columns, tokens, partners, counts, gain_query, gain_memory, w_query, w_key, w_value, w_out):
    own, tok, width = tokens.shape
    listed = partners.shape[1]
    ring = Ring(lax.axis_size("img"), columns)
    ahead, back, sibling = ring.onward(1), ring.onward(-1), ring.sibling()
    sizes = dict(own=own, tok=tok, width=width)
    send = lambda array, to: lax.ppermute(array, "img", to)

    far = ring.chips // 2
    assert ring.chips == 2 * far and own == 2
    up, down = send(tokens, ahead), send(tokens, back)
    behind = [((0, True, 1), [send(tokens, sibling)])]
    operands = (tokens, partners, counts, gain_query, gain_memory, w_query, w_key, w_value, w_out)
    operands = [pltpu.with_memory_space_constraint(array, pltpu.HBM) for array in operands]
    total, spread_q, w_kv, w_out_here, tokens_here, gain_here, picks, table = first_stage(
        ring, ((0, False, 1),), operands, listed=listed, **sizes
    )
    state = (spread_q, w_kv, gain_here, picks, table)
    for step in range(1, far):
        waited = [array for _, arrays in behind for array in arrays]
        up, down, total, waited = lax.optimization_barrier((up, down, total, waited))
        behind = [(slot, [array]) for (slot, _), array in zip(behind, waited)]
        work = behind + [((-step, False, 1), [up]), ((step, False, 1), [down])]
        behind = [((-step, True, 1), [send(up, sibling)]), ((step, True, 1), [send(down, sibling)])]
        if step + 1 < far:
            up, down = send(up, ahead), send(down, back)
        else:
            up, down = send(up[0], ahead), send(down[1], back)
        (total,) = later_stage(ring, work, state, (), total, **sizes)
    (total,) = later_stage(ring, behind + [((far, False, own), [up, down])], state, (), total, **sizes)
    work = [((far, True, own), [send(up, sibling), send(down, sibling)])]
    _, mixed = later_stage(ring, work, state, (w_out_here, tokens_here, counts), total, **sizes)
    return mixed


def solution(mesh):
    placed = (
        P(("groups", "img"), None, None),
        P(("groups", "img"), None),
        P(("groups", "img")),
        P(),
        P(),
        P(),
        P(),
        P(),
        P(),
    )
    columns = max(1, 4 // mesh.shape["groups"])
    return jax.shard_map(
        functools.partial(shards, columns),
        mesh=mesh,
        in_specs=placed,
        out_specs=P(("groups", "img"), None, None),
        check_vma=False,
    )
```

```python
import functools

import jax
import jax.numpy as jnp
from jax import lax
from jax.experimental import pallas as pl
from jax.experimental.pallas import tpu as pltpu
from jax.sharding import PartitionSpec as P

HEADS = 12
HEAD_DIM = 64
CORES = 2
LANES = 128
PAIRED = 2 * HEAD_DIM


class Ring:
    def __init__(self, devices, columns):
        self.chips = devices // CORES
        self.columns = columns
        self.rows = self.chips // columns

    def chip(self, place):
        if self.columns == 1:
            return place
        if place < self.rows:
            return place * 2
        return (2 * self.rows - 1 - place) * 2 + 1

    def onward(self, step):
        pairs = []
        for place in range(self.chips):
            for core, way in ((0, step), (1, -step)):
                target = self.chip((place + way) % self.chips)
                pairs.append((self.chip(place) * CORES + core, target * CORES + core))
        return pairs

    def sibling(self):
        return [(i, i ^ 1) for i in range(self.chips * CORES)]

    def owner(self, me, shift, flip):
        chip = me // CORES
        core = lax.rem(me, CORES)
        if flip:
            core = 1 - core
        if self.columns == 1:
            place = chip
        else:
            row = chip // 2
            place = jnp.where(lax.rem(chip, 2) == 0, row, 2 * self.rows - 1 - row)
        came = lax.rem(place + self.chips + jnp.where(core == 0, -shift, shift), self.chips)
        if self.columns == 1:
            there = came
        else:
            there = jnp.where(came < self.rows, came * 2, (2 * self.rows - 1 - came) * 2 + 1)
        return there * CORES + core


def normalize(rows, gain):
    rows = rows.astype(jnp.float32)
    center = rows - jnp.mean(rows, axis=-1, keepdims=True)
    spread = jnp.mean(center * center, axis=-1, keepdims=True)
    return center * lax.rsqrt(spread + 1e-06) * gain


def dot(a, b, dims=((1,), (0,))):
    return lax.dot_general(a, b, (dims, ((), ())), preferred_element_type=jnp.float32)


def find_slot(owner, partners, counts, own, listed):
    image = jnp.int32(0)
    index = jnp.int32(0)
    live = jnp.int32(0)
    for a in range(own):
        for k in range(listed):
            partner = partners[a, k]
            hit = jnp.logical_and(k < counts[a], partner // own == owner)
            image = jnp.where(hit, a, image)
            index = jnp.where(hit, lax.rem(partner, own), index)
            live = jnp.where(hit, 1, live)
    return image, index, live


def attend(memory, slots, gain, w_kv, spread_q, total, tok):
    width = memory.shape[-1]
    normed = normalize(memory, gain).astype(jnp.bfloat16)
    both = dot(normed, w_kv[...]).astype(jnp.bfloat16)
    for at, (image, live) in enumerate(slots):
        here = slice(at * tok, (at + 1) * tok)
        for g in range(HEADS // 2):
            feats = slice(g * PAIRED, (g + 1) * PAIRED)
            scores = dot(both[here, feats], spread_q[image, feats, :])
            weights = jnp.exp(scores - jnp.max(scores, axis=0, keepdims=True))
            share = live.astype(jnp.float32) / jnp.sum(weights, axis=0, keepdims=True)
            weights = weights.astype(jnp.bfloat16)
            parts = []
            for h in range(2):
                values = both[here, width + g * PAIRED + h * HEAD_DIM : width + g * PAIRED + (h + 1) * HEAD_DIM]
                asked = slice(h * tok, (h + 1) * tok)
                parts.append(dot(values, weights[:, asked], ((0,), (0,))) * share[:, asked])
            total[image, feats, :] += jnp.concatenate(parts, axis=0)


def first_kernel(ring, slots, own, listed, tok, *refs):
    (tokens, partners, counts, gain_query, gain_memory, w_query, w_key, w_value, w_out) = refs[:9]
    total, spread_q, w_kv, w_out_here, tokens_here, gain_here, picks, table = refs[9:17]
    partners_here, counts_here, gain_query_here, w_query_here, sems = refs[17:]
    width = tokens.shape[-1]
    copies = [
        pltpu.make_async_copy(source, target, sems.at[i])
        for i, (source, target) in enumerate(
            (
                (partners, partners_here),
                (counts, counts_here),
                (tokens, tokens_here),
                (gain_query, gain_query_here),
                (w_query, w_query_here),
                (gain_memory, gain_here),
                (w_key, w_kv.at[:, pl.ds(0, width)]),
                (w_value, w_kv.at[:, pl.ds(width, width)]),
                (w_out, w_out_here),
            )
        )
    ]
    for copy in copies:
        copy.start()
    total[...] = jnp.zeros_like(total)
    for copy in copies[:2]:
        copy.wait()
    for owner in range(ring.chips * CORES):
        image, index, live = find_slot(owner, partners_here, counts_here, own, listed)
        table[0, owner] = image
        table[1, owner] = live
        picks[owner : owner + 1, :] = jnp.full((1, LANES), index.astype(jnp.float32))
    for copy in copies[2:5]:
        copy.wait()
    rows = tokens_here[...].reshape(own * tok, -1)
    normed_query = normalize(rows, gain_query_here[...][None, :]).astype(jnp.bfloat16)
    queries = dot(normed_query, w_query_here[...]).astype(jnp.bfloat16).astype(jnp.float32)
    queries_t = (queries * (1.0 / HEAD_DIM**0.5)).T.astype(jnp.bfloat16)
    zero = jnp.zeros((HEAD_DIM, tok), jnp.bfloat16)
    for a in range(own):
        for h in range(HEADS):
            part = queries_t[h * HEAD_DIM : (h + 1) * HEAD_DIM, a * tok : (a + 1) * tok]
            pieces = [part, zero] if h % 2 == 0 else [zero, part]
            spread_q[a, h * HEAD_DIM : (h + 1) * HEAD_DIM, :] = jnp.concatenate(pieces, axis=1)
    for copy in copies[5:8]:
        copy.wait()
    me = lax.axis_index("img")
    chosen, asked = [], []
    for shift, flip, _ in slots:
        owner = ring.owner(me, shift, flip)
        chosen.append(choose([tokens_here[j] for j in range(own)], picks, owner))
        asked.append((table[0, owner], table[1, owner]))
    attend(jnp.concatenate(chosen, axis=0), asked, gain_here[...][None, :], w_kv, spread_q, total, tok)
    copies[8].wait()


def choose(images, picks, owner):
    width = images[0].shape[-1]
    pick = jnp.concatenate([picks[pl.ds(owner, 1), :]] * (width // LANES), axis=1)
    chosen = images[0].astype(jnp.float32)
    for j in range(1, len(images)):
        chosen = jnp.where(pick == j, images[j].astype(jnp.float32), chosen)
    return chosen


def later_kernel(ring, slots, passes, last, own, tok, *refs):
    refs = list(refs)
    take = lambda n: [refs.pop(0) for _ in range(n)]
    sources = [take(n) for _, _, n in slots]
    (arrived,) = take(1) if any(n == 0 for _, _, n in slots) else (None,)
    (sibling_picks,) = take(1) if passes else (None,)
    spread_q, w_kv, gain, picks, table, _ = take(6)
    if last:
        w_out, tokens, counts, total, mixed, counts_here, table_here, sems = refs
    else:
        (total,) = take(1)
        (passed,) = take(1) if passes else (None,)
        table_here, sems = refs
    copies = [pltpu.make_async_copy(table, table_here, sems.at[0])]
    if last:
        copies.append(pltpu.make_async_copy(counts, counts_here, sems.at[1]))
    for copy in copies:
        copy.start()
    me = lax.axis_index("img")
    owners = [ring.owner(me, shift, flip) for shift, flip, _ in slots]
    chosen = []
    came = sent = 0
    for (_, flip, _), arrays, owner in zip(slots, sources, owners):
        if not arrays:
            chosen.append(arrived[came].astype(jnp.float32))
            came += 1
            continue
        images = [arrays[0][j] for j in range(own)] if len(arrays) == 1 else [array[...] for array in arrays]
        chosen.append(choose(images, picks, owner))
        if passes and not flip:
            passed[sent] = choose(images, sibling_picks, owner).astype(passed.dtype)
            sent += 1
    for copy in copies:
        copy.wait()
    asked = [(table_here[0, owner], table_here[1, owner]) for owner in owners]
    attend(jnp.concatenate(chosen, axis=0), asked, gain[...][None, :], w_kv, spread_q, total, tok)
    if last:
        for a in range(own):
            context = (total[a] / counts_here[a].astype(jnp.float32)).T.astype(jnp.bfloat16)
            out = tokens[a].astype(jnp.float32) + dot(context, w_out[...])
            mixed[a] = out.astype(jnp.bfloat16)


HBM = pl.BlockSpec(memory_space=pltpu.HBM)
ANY = pl.BlockSpec(memory_space=pl.ANY)
SMEM = pl.BlockSpec(memory_space=pltpu.SMEM)
VMEM = pl.BlockSpec(memory_space=pltpu.VMEM)


def cost(rows, tok, width):
    return pl.CostEstimate(
        flops=4 * rows * width * (width + tok) * 2,
        bytes_accessed=2 * width * width * 2 + 3 * rows * width * 2,
        transcendentals=rows * tok * HEADS,
    )


def first_stage(ring, slots, operands, own, listed, tok, width):
    devices = ring.chips * CORES
    shapes = [
        jax.ShapeDtypeStruct((own, width, tok), jnp.float32),
        jax.ShapeDtypeStruct((own, width, 2 * tok), jnp.bfloat16),
        jax.ShapeDtypeStruct((width, 2 * width), jnp.bfloat16),
        jax.ShapeDtypeStruct((width, width), jnp.bfloat16),
        jax.ShapeDtypeStruct((own, tok, width), jnp.bfloat16),
        jax.ShapeDtypeStruct((width,), jnp.float32),
        jax.ShapeDtypeStruct((devices, LANES), jnp.float32),
        jax.ShapeDtypeStruct((2, devices), jnp.int32),
    ]
    return pl.pallas_call(
        functools.partial(first_kernel, ring, slots, own, listed, tok),
        out_shape=shapes,
        in_specs=[HBM] * len(operands),
        out_specs=[VMEM] * 7 + [SMEM],
        scratch_shapes=[
            pltpu.SMEM((own, listed), jnp.int32),
            pltpu.SMEM((own,), jnp.int32),
            pltpu.VMEM((width,), jnp.float32),
            pltpu.VMEM((width, width), jnp.bfloat16),
            pltpu.SemaphoreType.DMA((9,)),
        ],
        compiler_params=pltpu.CompilerParams(vmem_limit_bytes=32 << 20),
        cost_estimate=cost(own * tok, tok, width),
    )(*operands)


def later_stage(ring, work, arrived, sibling_picks, state, extra, total, own, tok, width):
    slots, sources = zip(*work)
    last, passes = len(extra) > 0, sibling_picks is not None
    images = [array for arrays in sources for array in arrays]
    images += [] if arrived is None else [arrived]
    images += [sibling_picks] if passes else []
    shapes = [jax.ShapeDtypeStruct(total.shape, total.dtype)]
    scratch = [pltpu.SMEM((2, ring.chips * CORES), jnp.int32), pltpu.SemaphoreType.DMA((2,))]
    if passes:
        shapes.append(jax.ShapeDtypeStruct((sum(not flip for _, flip, _ in slots), tok, width), jnp.bfloat16))
    if last:
        shapes.append(jax.ShapeDtypeStruct((own, tok, width), jnp.bfloat16))
        scratch = [pltpu.SMEM((own,), jnp.int32)] + scratch
    return pl.pallas_call(
        functools.partial(later_kernel, ring, slots, passes, last, own, tok),
        out_shape=shapes,
        in_specs=[VMEM] * (len(images) + 4) + [ANY, VMEM] + ([VMEM, VMEM, ANY] if last else []),
        out_specs=[VMEM] * len(shapes),
        scratch_shapes=scratch,
        input_output_aliases={len(images) + 5: 0},
        compiler_params=pltpu.CompilerParams(vmem_limit_bytes=32 << 20),
        cost_estimate=cost(len(slots) * tok, tok, width),
    )(*images, *state, total, *extra)


def shards(columns, tokens, partners, counts, gain_query, gain_memory, w_query, w_key, w_value, w_out):
    own, tok, width = tokens.shape
    listed = partners.shape[1]
    ring = Ring(lax.axis_size("img"), columns)
    ahead, back, sibling = ring.onward(1), ring.onward(-1), ring.sibling()
    sizes = dict(own=own, tok=tok, width=width)
    send = lambda array, to: lax.ppermute(array, "img", to)

    far = ring.chips // 2
    assert ring.chips == 2 * far and own == 2
    up, down = send(tokens, ahead), send(tokens, back)
    arrived = send(tokens, sibling)
    operands = (tokens, partners, counts, gain_query, gain_memory, w_query, w_key, w_value, w_out)
    operands = [pltpu.with_memory_space_constraint(array, pltpu.HBM) for array in operands]
    total, spread_q, w_kv, w_out_here, tokens_here, gain_here, picks, table = first_stage(
        ring, ((0, False, 1),), operands, listed=listed, **sizes
    )
    sibling_picks = send(picks, sibling)
    state = (spread_q, w_kv, gain_here, picks, table)
    behind = [((0, True, 1), [arrived])]
    arrived = None
    for step in range(1, far):
        up, down, total = lax.optimization_barrier((up, down, total))
        work = behind + [((step, False, 1), [up]), ((-step, False, 1), [down])]
        if step + 1 < far:
            up, down = send(up, ahead), send(down, back)
        else:
            up = send(up, ahead)
        total, passed = later_stage(ring, work, arrived, sibling_picks, state, (), total, **sizes)
        arrived = send(passed, sibling)
        behind = [((step, True, 0), []), ((-step, True, 0), [])]
    work = behind + [((far, False, 1), [up])]
    (total,) = later_stage(ring, work, arrived, None, state, (), total, **sizes)
    work = [((far, True, 1), [send(up, sibling)])]
    _, mixed = later_stage(ring, work, None, None, state, (w_out_here, tokens_here, counts), total, **sizes)
    return mixed


def solution(mesh):
    placed = (
        P(("groups", "img"), None, None),
        P(("groups", "img"), None),
        P(("groups", "img")),
        P(),
        P(),
        P(),
        P(),
        P(),
        P(),
    )
    columns = max(1, 4 // mesh.shape["groups"])
    return jax.shard_map(
        functools.partial(shards, columns),
        mesh=mesh,
        in_specs=placed,
        out_specs=P(("groups", "img"), None, None),
        check_vma=False,
    )
```

```python
import functools

import jax
import jax.numpy as jnp
from jax import lax
from jax.experimental import pallas as pl
from jax.experimental.pallas import tpu as pltpu
from jax.sharding import PartitionSpec as P

HEADS = 12
HEAD_DIM = 64
CORES = 2
LANES = 128
PAIRED = 2 * HEAD_DIM


class Ring:
    def __init__(self, devices, columns):
        self.chips = devices // CORES
        self.columns = columns
        self.rows = self.chips // columns

    def chip(self, place):
        if self.columns == 1:
            return place
        if place < self.rows:
            return place * 2
        return (2 * self.rows - 1 - place) * 2 + 1

    def onward(self, step):
        pairs = []
        for place in range(self.chips):
            for core, way in ((0, step), (1, -step)):
                target = self.chip((place + way) % self.chips)
                pairs.append((self.chip(place) * CORES + core, target * CORES + core))
        return pairs

    def sibling(self):
        return [(i, i ^ 1) for i in range(self.chips * CORES)]

    def pairs(self):
        return [[chip * CORES + core for core in range(CORES)] for chip in range(self.chips)]

    def owner(self, me, shift, flip):
        chip = me // CORES
        core = lax.rem(me, CORES)
        if flip:
            core = 1 - core
        if self.columns == 1:
            place = chip
        else:
            row = chip // 2
            place = jnp.where(lax.rem(chip, 2) == 0, row, 2 * self.rows - 1 - row)
        came = lax.rem(place + self.chips + jnp.where(core == 0, -shift, shift), self.chips)
        if self.columns == 1:
            there = came
        else:
            there = jnp.where(came < self.rows, came * 2, (2 * self.rows - 1 - came) * 2 + 1)
        return there * CORES + core


def normalize(rows, gain):
    rows = rows.astype(jnp.float32)
    center = rows - jnp.mean(rows, axis=-1, keepdims=True)
    spread = jnp.mean(center * center, axis=-1, keepdims=True)
    return center * lax.rsqrt(spread + 1e-06) * gain


def dot(a, b, dims=((1,), (0,))):
    return lax.dot_general(a, b, (dims, ((), ())), preferred_element_type=jnp.float32)


def find_slot(owner, partners, counts, own, listed):
    image = jnp.int32(0)
    index = jnp.int32(0)
    live = jnp.int32(0)
    for a in range(own):
        for k in range(listed):
            partner = partners[a, k]
            hit = jnp.logical_and(k < counts[a], partner // own == owner)
            image = jnp.where(hit, a, image)
            index = jnp.where(hit, lax.rem(partner, own), index)
            live = jnp.where(hit, 1, live)
    return image, index, live


def attend(memory, find_slots, gain, w_kv, spread_q, total, tok):
    width = memory.shape[-1]
    normed = normalize(memory, gain).astype(jnp.bfloat16)
    both = dot(normed, w_kv[...]).astype(jnp.bfloat16)
    for at, (image, live) in enumerate(find_slots()):
        here = slice(at * tok, (at + 1) * tok)
        for g in range(HEADS // 2):
            feats = slice(g * PAIRED, (g + 1) * PAIRED)
            scores = dot(both[here, feats], spread_q[image, feats, :])
            weights = jnp.exp(scores - jnp.max(scores, axis=0, keepdims=True))
            share = live.astype(jnp.float32) / jnp.sum(weights, axis=0, keepdims=True)
            weights = weights.astype(jnp.bfloat16)
            parts = []
            for h in range(2):
                values = both[here, width + g * PAIRED + h * HEAD_DIM : width + g * PAIRED + (h + 1) * HEAD_DIM]
                asked = slice(h * tok, (h + 1) * tok)
                parts.append(dot(values, weights[:, asked], ((0,), (0,))) * share[:, asked])
            total[image, feats, :] += jnp.concatenate(parts, axis=0)


def first_kernel(ring, slots, own, listed, tok, *refs):
    (tokens, partners, counts, gain_query, gain_memory, w_query, w_key, w_value, w_out) = refs[:9]
    total, spread_q, w_kv, w_out_here, tokens_here, gain_here, picks, table = refs[9:17]
    partners_here, counts_here, gain_query_here, w_query_here, sems = refs[17:]
    width = tokens.shape[-1]
    copies = [
        pltpu.make_async_copy(source, target, sems.at[i])
        for i, (source, target) in enumerate(
            (
                (partners, partners_here),
                (counts, counts_here),
                (tokens, tokens_here),
                (gain_query, gain_query_here),
                (w_query, w_query_here),
                (gain_memory, gain_here),
                (w_key, w_kv.at[:, pl.ds(0, width)]),
                (w_value, w_kv.at[:, pl.ds(width, width)]),
                (w_out, w_out_here),
            )
        )
    ]
    for copy in copies:
        copy.start()
    total[...] = jnp.zeros_like(total)
    for copy in copies[:2]:
        copy.wait()
    for owner in range(ring.chips * CORES):
        image, index, live = find_slot(owner, partners_here, counts_here, own, listed)
        table[0, owner] = image
        table[1, owner] = live
        picks[owner : owner + 1, :] = jnp.full((1, LANES), index.astype(jnp.float32))
    for copy in copies[2:5]:
        copy.wait()
    rows = tokens_here[...].reshape(own * tok, -1)
    normed_query = normalize(rows, gain_query_here[...][None, :]).astype(jnp.bfloat16)
    queries = dot(normed_query, w_query_here[...]).astype(jnp.bfloat16).astype(jnp.float32)
    queries_t = (queries * (1.0 / HEAD_DIM**0.5)).T.astype(jnp.bfloat16)
    zero = jnp.zeros((HEAD_DIM, tok), jnp.bfloat16)
    for a in range(own):
        for h in range(HEADS):
            part = queries_t[h * HEAD_DIM : (h + 1) * HEAD_DIM, a * tok : (a + 1) * tok]
            pieces = [part, zero] if h % 2 == 0 else [zero, part]
            spread_q[a, h * HEAD_DIM : (h + 1) * HEAD_DIM, :] = jnp.concatenate(pieces, axis=1)
    for copy in copies[5:8]:
        copy.wait()
    me = lax.axis_index("img")
    chosen, asked = [], []
    for shift, flip, _ in slots:
        owner = ring.owner(me, shift, flip)
        chosen.append(choose([tokens_here[j] for j in range(own)], picks, owner))
        asked.append((table[0, owner], table[1, owner]))
    attend(jnp.concatenate(chosen, axis=0), lambda: asked, gain_here[...][None, :], w_kv, spread_q, total, tok)
    copies[8].wait()


def choose(images, picks, owner):
    width = images[0].shape[-1]
    pick = jnp.concatenate([picks[pl.ds(owner, 1), :]] * (width // LANES), axis=1)
    chosen = images[0].astype(jnp.float32)
    for j in range(1, len(images)):
        chosen = jnp.where(pick == j, images[j].astype(jnp.float32), chosen)
    return chosen


def later_kernel(ring, slots, last, own, tok, *refs):
    refs = list(refs)
    take = lambda n: [refs.pop(0) for _ in range(n)]
    sources = [take(n) for _, _, n in slots]
    (arrived,) = take(1) if any(n == 0 for _, _, n in slots) else (None,)
    spread_q, w_kv, gain, picks, table, _ = take(6)
    if last:
        w_out, tokens, counts, total, mixed, counts_here, table_here, sems = refs
    else:
        total, table_here, sems = refs
    copies = [pltpu.make_async_copy(table, table_here, sems.at[0])]
    if last:
        copies.append(pltpu.make_async_copy(counts, counts_here, sems.at[1]))
    for copy in copies:
        copy.start()
    me = lax.axis_index("img")
    owners = [ring.owner(me, shift, flip) for shift, flip, _ in slots]
    chosen = []
    came = 0
    other = 1 - lax.rem(me, CORES)
    for (_, flip, _), arrays, owner in zip(slots, sources, owners):
        if arrays and len(arrays[0].shape) == 2:
            chosen.append(arrays[0][...].astype(jnp.float32))
            continue
        if not arrays:
            chosen.append(arrived[other, came].astype(jnp.float32))
            came += 1
            continue
        images = [arrays[0][j] for j in range(own)]
        chosen.append(choose(images, picks, owner))

    def find_slots():
        for copy in copies:
            copy.wait()
        return [(table_here[0, owner], table_here[1, owner]) for owner in owners]

    attend(jnp.concatenate(chosen, axis=0), find_slots, gain[...][None, :], w_kv, spread_q, total, tok)
    if last:
        context = jnp.concatenate([total[a] / counts_here[a].astype(jnp.float32) for a in range(own)], axis=1)
        out = dot(context.astype(jnp.bfloat16), w_out[...], ((0,), (0,)))
        mixed[...] = (tokens[...].astype(jnp.float32) + out.reshape(tokens.shape)).astype(jnp.bfloat16)


HBM = pl.BlockSpec(memory_space=pltpu.HBM)
ANY = pl.BlockSpec(memory_space=pl.ANY)
SMEM = pl.BlockSpec(memory_space=pltpu.SMEM)
VMEM = pl.BlockSpec(memory_space=pltpu.VMEM)


def cost(rows, tok, width):
    return pl.CostEstimate(
        flops=rows * width,
        bytes_accessed=rows * width,
        transcendentals=rows,
    )


def first_stage(ring, slots, operands, own, listed, tok, width):
    devices = ring.chips * CORES
    shapes = [
        jax.ShapeDtypeStruct((own, width, tok), jnp.float32),
        jax.ShapeDtypeStruct((own, width, 2 * tok), jnp.bfloat16),
        jax.ShapeDtypeStruct((width, 2 * width), jnp.bfloat16),
        jax.ShapeDtypeStruct((width, width), jnp.bfloat16),
        jax.ShapeDtypeStruct((own, tok, width), jnp.bfloat16),
        jax.ShapeDtypeStruct((width,), jnp.float32),
        jax.ShapeDtypeStruct((devices, LANES), jnp.float32),
        jax.ShapeDtypeStruct((2, devices), jnp.int32),
    ]
    return pl.pallas_call(
        functools.partial(first_kernel, ring, slots, own, listed, tok),
        out_shape=shapes,
        in_specs=[HBM] * len(operands),
        out_specs=[VMEM] * 7 + [SMEM],
        scratch_shapes=[
            pltpu.SMEM((own, listed), jnp.int32),
            pltpu.SMEM((own,), jnp.int32),
            pltpu.VMEM((width,), jnp.float32),
            pltpu.VMEM((width, width), jnp.bfloat16),
            pltpu.SemaphoreType.DMA((9,)),
        ],
        compiler_params=pltpu.CompilerParams(vmem_limit_bytes=32 << 20),
        cost_estimate=cost(own * tok, tok, width),
    )(*operands)


def later_stage(ring, work, arrived, state, extra, total, own, tok, width):
    slots, sources = zip(*work)
    last = len(extra) > 0
    images = [array for arrays in sources for array in arrays]
    images += [] if arrived is None else [arrived]
    shapes = [jax.ShapeDtypeStruct(total.shape, total.dtype)]
    scratch = [pltpu.SMEM((2, ring.chips * CORES), jnp.int32), pltpu.SemaphoreType.DMA((2,))]
    if last:
        shapes.append(jax.ShapeDtypeStruct((own, tok, width), jnp.bfloat16))
        scratch = [pltpu.SMEM((own,), jnp.int32)] + scratch
    return pl.pallas_call(
        functools.partial(later_kernel, ring, slots, last, own, tok),
        out_shape=shapes,
        in_specs=[VMEM] * (len(images) + 4) + [ANY, VMEM] + ([VMEM, VMEM, ANY] if last else []),
        out_specs=[VMEM] * len(shapes),
        scratch_shapes=scratch,
        input_output_aliases={len(images) + 5: 0},
        compiler_params=pltpu.CompilerParams(vmem_limit_bytes=32 << 20),
        cost_estimate=cost(len(slots) * tok, tok, width),
    )(*images, *state, total, *extra)


def pass_kernel(ring, wanted, own, *refs):
    arrays, picks, passed = refs[: len(wanted)], refs[len(wanted) : 2 * len(wanted)], refs[2 * len(wanted) :]
    me = lax.axis_index("img")
    for i, shift in enumerate(wanted):
        images = [arrays[i][j] for j in range(own)]
        chosen = choose(images, picks[i], ring.owner(me, shift, False)).astype(jnp.bfloat16)
        if len(passed) == 1:
            passed[0][i] = chosen
        else:
            passed[i][...] = chosen


def pass_stage(ring, work, together, own, tok, width):
    wanted, arrays, picks = zip(*work)
    if together:
        shapes = jax.ShapeDtypeStruct((len(work), tok, width), jnp.bfloat16)
    else:
        shapes = [jax.ShapeDtypeStruct((tok, width), jnp.bfloat16)] * len(work)
    return pl.pallas_call(
        functools.partial(pass_kernel, ring, wanted, own),
        out_shape=shapes,
        in_specs=[VMEM] * (2 * len(work)),
        out_specs=VMEM if together else [VMEM] * len(work),
        compiler_params=pltpu.CompilerParams(vmem_limit_bytes=32 << 20),
        cost_estimate=pl.CostEstimate(
            flops=len(work) * own * tok * width, bytes_accessed=len(work) * own * tok * width * 2, transcendentals=0
        ),
    )(*arrays, *picks)


def shards(columns, tokens, partners, counts, gain_query, gain_memory, w_query, w_key, w_value, w_out):
    own, tok, width = tokens.shape
    listed = partners.shape[1]
    ring = Ring(lax.axis_size("img"), columns)
    ahead, back, sibling = ring.onward(1), ring.onward(-1), ring.sibling()
    sizes = dict(own=own, tok=tok, width=width)
    send = lambda array, to: lax.ppermute(array, "img", to)

    far = ring.chips // 2
    assert ring.chips == 2 * far and far > 1 and own == 2
    up, down, theirs = send(tokens, ahead), send(tokens, back), send(tokens, sibling)
    meet = lambda array: lax.all_gather(array, "img", axis_index_groups=ring.pairs())
    operands = (tokens, partners, counts, gain_query, gain_memory, w_query, w_key, w_value, w_out)
    operands = [pltpu.with_memory_space_constraint(array, pltpu.HBM) for array in operands]
    total, spread_q, w_kv, w_out_here, tokens_here, gain_here, picks, table = first_stage(
        ring, ((0, False, 1),), operands, listed=listed, **sizes
    )
    cross = [(source, target ^ 1) for source, target in ahead]
    sibling_picks = send(picks, sibling)
    next_picks, cross_picks = send(picks, back), send(picks, [(target, source) for source, target in cross])
    state = (spread_q, w_kv, gain_here, picks, table)
    behind = [((0, True, 1), [theirs])]
    for step in range(1, far):
        down, total = lax.optimization_barrier((down, total))
        work = [((step, False, 1), [up]), ((-step, False, 1), [down])]
        passed = pass_stage(ring, [(step, up, sibling_picks), (-step, down, sibling_picks)], True, **sizes)
        if step + 1 < far:
            up, down = send(up, ahead), send(down, back)
        else:
            same, other = pass_stage(ring, [(step, up, next_picks), (step, up, cross_picks)], False, **sizes)
            same, other = send(same, ahead), send(other, cross)
        work += behind + [((step, True, 0), []), ((-step, True, 0), [])]
        (total,) = later_stage(ring, work, meet(passed), state, (), total, **sizes)
        behind = []
    work = [((far, False, 1), [same]), ((far, True, 1), [other])]
    _, mixed = later_stage(ring, work, None, state, (w_out_here, tokens_here, counts), total, **sizes)
    return mixed


def solution(mesh):
    placed = (
        P(("groups", "img"), None, None),
        P(("groups", "img"), None),
        P(("groups", "img")),
        P(),
        P(),
        P(),
        P(),
        P(),
        P(),
    )
    columns = max(1, 4 // mesh.shape["groups"])
    return jax.shard_map(
        functools.partial(shards, columns),
        mesh=mesh,
        in_specs=placed,
        out_specs=P(("groups", "img"), None, None),
        check_vma=False,
    )
```

```python
import functools

import jax
import jax.numpy as jnp
from jax import lax
from jax.experimental import pallas as pl
from jax.experimental.pallas import tpu as pltpu
from jax.sharding import PartitionSpec as P

HEADS = 12
HEAD_DIM = 64
CORES = 2
LANES = 128
PAIRED = 2 * HEAD_DIM


class Ring:
    def __init__(self, devices, columns):
        self.chips = devices // CORES
        self.columns = columns
        self.rows = self.chips // columns

    def chip(self, place):
        if self.columns == 1:
            return place
        if place < self.rows:
            return place * 2
        return (2 * self.rows - 1 - place) * 2 + 1

    def onward(self, step):
        pairs = []
        for place in range(self.chips):
            for core, way in ((0, step), (1, -step)):
                target = self.chip((place + way) % self.chips)
                pairs.append((self.chip(place) * CORES + core, target * CORES + core))
        return pairs

    def sibling(self):
        return [(i, i ^ 1) for i in range(self.chips * CORES)]

    def pairs(self):
        return [[chip * CORES + core for core in range(CORES)] for chip in range(self.chips)]

    def owner(self, me, shift, flip):
        chip = me // CORES
        core = lax.rem(me, CORES)
        if flip:
            core = 1 - core
        if self.columns == 1:
            place = chip
        else:
            row = chip // 2
            place = jnp.where(lax.rem(chip, 2) == 0, row, 2 * self.rows - 1 - row)
        came = lax.rem(place + self.chips + jnp.where(core == 0, -shift, shift), self.chips)
        if self.columns == 1:
            there = came
        else:
            there = jnp.where(came < self.rows, came * 2, (2 * self.rows - 1 - came) * 2 + 1)
        return there * CORES + core


def normalize(rows, gain):
    rows = rows.astype(jnp.float32)
    center = rows - jnp.mean(rows, axis=-1, keepdims=True)
    spread = jnp.mean(center * center, axis=-1, keepdims=True)
    return center * lax.rsqrt(spread + 1e-06) * gain


def dot(a, b, dims=((1,), (0,))):
    return lax.dot_general(a, b, (dims, ((), ())), preferred_element_type=jnp.float32)


def find_slot(owner, partners, counts, own, listed):
    image = jnp.int32(0)
    index = jnp.int32(0)
    live = jnp.int32(0)
    for a in range(own):
        for k in range(listed):
            partner = partners[a, k]
            hit = jnp.logical_and(k < counts[a], partner // own == owner)
            image = jnp.where(hit, a, image)
            index = jnp.where(hit, lax.rem(partner, own), index)
            live = jnp.where(hit, 1, live)
    return image, index, live


def attend(memory, find_slots, gain, w_kv, spread_q, total, tok):
    width = memory.shape[-1]
    normed = normalize(memory, gain).astype(jnp.bfloat16)
    both = dot(normed, w_kv[...]).astype(jnp.bfloat16)
    for at, (image, live) in enumerate(find_slots()):
        here = slice(at * tok, (at + 1) * tok)
        for g in range(HEADS // 2):
            feats = slice(g * PAIRED, (g + 1) * PAIRED)
            scores = dot(both[here, feats], spread_q[image, feats, :])
            weights = jnp.exp(scores - jnp.max(scores, axis=0, keepdims=True))
            share = live.astype(jnp.float32) / jnp.sum(weights, axis=0, keepdims=True)
            weights = weights.astype(jnp.bfloat16)
            values = both[here, width + g * PAIRED : width + (g + 1) * PAIRED]
            crossed = dot(values, weights, ((0,), (0,)))
            first = crossed[:HEAD_DIM, :tok] * share[:, :tok]
            second = crossed[HEAD_DIM:, tok:] * share[:, tok:]
            total[image, feats, :] += jnp.concatenate([first, second], axis=0)


def first_kernel(ring, slots, own, listed, tok, *refs):
    (tokens, partners, counts, gain_query, gain_memory, w_query, w_key, w_value, w_out) = refs[:9]
    total, spread_q, w_kv, w_out_here, tokens_here, gain_here, picks, table = refs[9:17]
    partners_here, counts_here, gain_query_here, w_query_here, sems = refs[17:]
    width = tokens.shape[-1]
    copies = [
        pltpu.make_async_copy(source, target, sems.at[i])
        for i, (source, target) in enumerate(
            (
                (partners, partners_here),
                (counts, counts_here),
                (tokens, tokens_here),
                (gain_query, gain_query_here),
                (w_query, w_query_here),
                (gain_memory, gain_here),
                (w_key, w_kv.at[:, pl.ds(0, width)]),
                (w_value, w_kv.at[:, pl.ds(width, width)]),
                (w_out, w_out_here),
            )
        )
    ]
    for copy in copies:
        copy.start()
    total[...] = jnp.zeros_like(total)
    for copy in copies[:2]:
        copy.wait()
    for owner in range(ring.chips * CORES):
        image, index, live = find_slot(owner, partners_here, counts_here, own, listed)
        table[0, owner] = image
        table[1, owner] = live
        picks[owner : owner + 1, :] = jnp.full((1, LANES), index.astype(jnp.float32))
    for copy in copies[2:5]:
        copy.wait()
    rows = tokens_here[...].reshape(own * tok, -1)
    normed_query = normalize(rows, gain_query_here[...][None, :]).astype(jnp.bfloat16)
    queries = dot(normed_query, w_query_here[...]).astype(jnp.bfloat16).astype(jnp.float32)
    queries_t = (queries * (1.0 / HEAD_DIM**0.5)).T.astype(jnp.bfloat16)
    zero = jnp.zeros((HEAD_DIM, tok), jnp.bfloat16)
    for a in range(own):
        for h in range(HEADS):
            part = queries_t[h * HEAD_DIM : (h + 1) * HEAD_DIM, a * tok : (a + 1) * tok]
            pieces = [part, zero] if h % 2 == 0 else [zero, part]
            spread_q[a, h * HEAD_DIM : (h + 1) * HEAD_DIM, :] = jnp.concatenate(pieces, axis=1)
    for copy in copies[5:8]:
        copy.wait()
    me = lax.axis_index("img")
    chosen, asked = [], []
    for shift, flip, _ in slots:
        owner = ring.owner(me, shift, flip)
        chosen.append(choose([tokens_here[j] for j in range(own)], picks, owner))
        asked.append((table[0, owner], table[1, owner]))
    attend(jnp.concatenate(chosen, axis=0), lambda: asked, gain_here[...][None, :], w_kv, spread_q, total, tok)
    copies[8].wait()


def choose(images, picks, owner):
    width = images[0].shape[-1]
    pick = jnp.concatenate([picks[pl.ds(owner, 1), :]] * (width // LANES), axis=1)
    chosen = images[0].astype(jnp.float32)
    for j in range(1, len(images)):
        chosen = jnp.where(pick == j, images[j].astype(jnp.float32), chosen)
    return chosen


def later_kernel(ring, slots, last, own, tok, *refs):
    refs = list(refs)
    take = lambda n: [refs.pop(0) for _ in range(n)]
    sources = [take(n) for _, _, n in slots]
    (arrived,) = take(1) if any(n == 0 for _, _, n in slots) else (None,)
    spread_q, w_kv, gain, picks, table, _ = take(6)
    if last:
        w_out, tokens, counts, total, mixed, mixed_here, counts_here, table_here, sems = refs
    else:
        total, table_here, sems = refs
    copies = [pltpu.make_async_copy(table, table_here, sems.at[0])]
    if last:
        copies.append(pltpu.make_async_copy(counts, counts_here, sems.at[1]))
    for copy in copies:
        copy.start()
    me = lax.axis_index("img")
    owners = [ring.owner(me, shift, flip) for shift, flip, _ in slots]
    chosen = []
    came = 0
    other = 1 - lax.rem(me, CORES)
    for (_, flip, _), arrays, owner in zip(slots, sources, owners):
        if arrays and len(arrays[0].shape) == 2:
            chosen.append(arrays[0][...].astype(jnp.float32))
            continue
        if not arrays:
            chosen.append(arrived[other, came].astype(jnp.float32))
            came += 1
            continue
        images = [arrays[0][j] for j in range(own)]
        chosen.append(choose(images, picks, owner))

    def find_slots():
        for copy in copies:
            copy.wait()
        return [(table_here[0, owner], table_here[1, owner]) for owner in owners]

    attend(jnp.concatenate(chosen, axis=0), find_slots, gain[...][None, :], w_kv, spread_q, total, tok)
    if last:
        context = jnp.concatenate([total[a] / counts_here[a].astype(jnp.float32) for a in range(own)], axis=1)
        context = context.astype(jnp.bfloat16)
        half = tokens.shape[-1] // 2
        copies = []
        for i in range(2):
            part = pl.ds(i * half, half)
            out = dot(context, w_out[:, part], ((0,), (0,)))
            mixed_here[:, :, part] = (tokens[:, :, part].astype(jnp.float32) + out.reshape(own, tok, half)).astype(jnp.bfloat16)
            copies.append(pltpu.make_async_copy(mixed_here.at[:, :, part], mixed.at[:, :, part], sems.at[i]))
            copies[-1].start()
        for copy in copies:
            copy.wait()


HBM = pl.BlockSpec(memory_space=pltpu.HBM)
ANY = pl.BlockSpec(memory_space=pl.ANY)
SMEM = pl.BlockSpec(memory_space=pltpu.SMEM)
VMEM = pl.BlockSpec(memory_space=pltpu.VMEM)


def cost(rows, tok, width):
    return pl.CostEstimate(
        flops=rows * width,
        bytes_accessed=rows * width,
        transcendentals=rows,
    )


def first_stage(ring, slots, operands, own, listed, tok, width):
    devices = ring.chips * CORES
    shapes = [
        jax.ShapeDtypeStruct((own, width, tok), jnp.float32),
        jax.ShapeDtypeStruct((own, width, 2 * tok), jnp.bfloat16),
        jax.ShapeDtypeStruct((width, 2 * width), jnp.bfloat16),
        jax.ShapeDtypeStruct((width, width), jnp.bfloat16),
        jax.ShapeDtypeStruct((own, tok, width), jnp.bfloat16),
        jax.ShapeDtypeStruct((width,), jnp.float32),
        jax.ShapeDtypeStruct((devices, LANES), jnp.float32),
        jax.ShapeDtypeStruct((2, devices), jnp.int32),
    ]
    return pl.pallas_call(
        functools.partial(first_kernel, ring, slots, own, listed, tok),
        out_shape=shapes,
        in_specs=[HBM] * len(operands),
        out_specs=[VMEM] * 7 + [SMEM],
        scratch_shapes=[
            pltpu.SMEM((own, listed), jnp.int32),
            pltpu.SMEM((own,), jnp.int32),
            pltpu.VMEM((width,), jnp.float32),
            pltpu.VMEM((width, width), jnp.bfloat16),
            pltpu.SemaphoreType.DMA((9,)),
        ],
        compiler_params=pltpu.CompilerParams(vmem_limit_bytes=32 << 20),
        cost_estimate=cost(own * tok, tok, width),
    )(*operands)


def later_stage(ring, work, arrived, state, extra, total, own, tok, width):
    slots, sources = zip(*work)
    last = len(extra) > 0
    images = [array for arrays in sources for array in arrays]
    images += [] if arrived is None else [arrived]
    shapes = [jax.ShapeDtypeStruct(total.shape, total.dtype)]
    scratch = [pltpu.SMEM((2, ring.chips * CORES), jnp.int32), pltpu.SemaphoreType.DMA((2,))]
    if last:
        shapes.append(jax.ShapeDtypeStruct((own, tok, width), jnp.bfloat16))
        scratch = [pltpu.VMEM((own, tok, width), jnp.bfloat16), pltpu.SMEM((own,), jnp.int32)] + scratch
    return pl.pallas_call(
        functools.partial(later_kernel, ring, slots, last, own, tok),
        out_shape=shapes,
        in_specs=[VMEM] * (len(images) + 4) + [ANY, VMEM] + ([VMEM, VMEM, ANY] if last else []),
        out_specs=[VMEM] + ([HBM] if last else []),
        scratch_shapes=scratch,
        input_output_aliases={len(images) + 5: 0},
        compiler_params=pltpu.CompilerParams(vmem_limit_bytes=32 << 20),
        cost_estimate=cost(len(slots) * tok, tok, width),
    )(*images, *state, total, *extra)


def pass_kernel(ring, wanted, own, *refs):
    arrays, picks, passed = refs[: len(wanted)], refs[len(wanted) : 2 * len(wanted)], refs[2 * len(wanted) :]
    me = lax.axis_index("img")
    for i, shift in enumerate(wanted):
        images = [arrays[i][j] for j in range(own)]
        chosen = choose(images, picks[i], ring.owner(me, shift, False)).astype(jnp.bfloat16)
        if len(passed) == 1:
            passed[0][i] = chosen
        else:
            passed[i][...] = chosen


def pass_stage(ring, work, together, own, tok, width):
    wanted, arrays, picks = zip(*work)
    if together:
        shapes = jax.ShapeDtypeStruct((len(work), tok, width), jnp.bfloat16)
    else:
        shapes = [jax.ShapeDtypeStruct((tok, width), jnp.bfloat16)] * len(work)
    return pl.pallas_call(
        functools.partial(pass_kernel, ring, wanted, own),
        out_shape=shapes,
        in_specs=[VMEM] * (2 * len(work)),
        out_specs=VMEM if together else [VMEM] * len(work),
        compiler_params=pltpu.CompilerParams(vmem_limit_bytes=32 << 20),
        cost_estimate=pl.CostEstimate(
            flops=len(work) * own * tok * width, bytes_accessed=len(work) * own * tok * width * 2, transcendentals=0
        ),
    )(*arrays, *picks)


def shards(columns, tokens, partners, counts, gain_query, gain_memory, w_query, w_key, w_value, w_out):
    own, tok, width = tokens.shape
    listed = partners.shape[1]
    ring = Ring(lax.axis_size("img"), columns)
    ahead, back, sibling = ring.onward(1), ring.onward(-1), ring.sibling()
    sizes = dict(own=own, tok=tok, width=width)
    send = lambda array, to: lax.ppermute(array, "img", to)

    far = ring.chips // 2
    assert ring.chips == 2 * far and far > 1 and own == 2
    up, down, theirs = send(tokens, ahead), send(tokens, back), send(tokens, sibling)
    meet = lambda array: lax.all_gather(array, "img", axis_index_groups=ring.pairs())
    operands = (tokens, partners, counts, gain_query, gain_memory, w_query, w_key, w_value, w_out)
    operands = [pltpu.with_memory_space_constraint(array, pltpu.HBM) for array in operands]
    total, spread_q, w_kv, w_out_here, tokens_here, gain_here, picks, table = first_stage(
        ring, ((0, False, 1),), operands, listed=listed, **sizes
    )
    cross = [(source, target ^ 1) for source, target in ahead]
    sibling_picks = send(picks, sibling)
    next_picks, cross_picks = send(picks, back), send(picks, [(target, source) for source, target in cross])
    state = (spread_q, w_kv, gain_here, picks, table)
    behind = [((0, True, 1), [theirs])]
    for step in range(1, far):
        down, total = lax.optimization_barrier((down, total))
        work = [((step, False, 1), [up]), ((-step, False, 1), [down])]
        passed = pass_stage(ring, [(step, up, sibling_picks), (-step, down, sibling_picks)], True, **sizes)
        if step + 1 < far:
            up, down = send(up, ahead), send(down, back)
        else:
            same, other = pass_stage(ring, [(step, up, next_picks), (step, up, cross_picks)], False, **sizes)
            same, other = send(same, ahead), send(other, cross)
        work += behind + [((step, True, 0), []), ((-step, True, 0), [])]
        (total,) = later_stage(ring, work, meet(passed), state, (), total, **sizes)
        behind = []
    work = [((far, False, 1), [same]), ((far, True, 1), [other])]
    _, mixed = later_stage(ring, work, None, state, (w_out_here, tokens_here, counts), total, **sizes)
    return mixed


def solution(mesh):
    placed = (
        P(("groups", "img"), None, None),
        P(("groups", "img"), None),
        P(("groups", "img")),
        P(),
        P(),
        P(),
        P(),
        P(),
        P(),
    )
    columns = max(1, 4 // mesh.shape["groups"])
    return jax.shard_map(
        functools.partial(shards, columns),
        mesh=mesh,
        in_specs=placed,
        out_specs=P(("groups", "img"), None, None),
        check_vma=False,
    )
```

```python
import functools

import jax
import jax.numpy as jnp
from jax import lax
from jax.experimental import pallas as pl
from jax.experimental.pallas import tpu as pltpu
from jax.sharding import PartitionSpec as P

HEADS = 12
HEAD_DIM = 64
CORES = 2
LANES = 128
PAIRED = 2 * HEAD_DIM


class Ring:
    def __init__(self, devices, columns):
        self.chips = devices // CORES
        self.columns = columns
        self.rows = self.chips // columns

    def chip(self, place):
        if self.columns == 1:
            return place
        if place < self.rows:
            return place * 2
        return (2 * self.rows - 1 - place) * 2 + 1

    def onward(self, step):
        pairs = []
        for place in range(self.chips):
            for core, way in ((0, step), (1, -step)):
                target = self.chip((place + way) % self.chips)
                pairs.append((self.chip(place) * CORES + core, target * CORES + core))
        return pairs

    def sibling(self):
        return [(i, i ^ 1) for i in range(self.chips * CORES)]

    def pairs(self):
        return [[chip * CORES + core for core in range(CORES)] for chip in range(self.chips)]

    def owner(self, me, shift, flip):
        chip = me // CORES
        core = lax.rem(me, CORES)
        if flip:
            core = 1 - core
        if self.columns == 1:
            place = chip
        else:
            row = chip // 2
            place = jnp.where(lax.rem(chip, 2) == 0, row, 2 * self.rows - 1 - row)
        came = lax.rem(place + self.chips + jnp.where(core == 0, -shift, shift), self.chips)
        if self.columns == 1:
            there = came
        else:
            there = jnp.where(came < self.rows, came * 2, (2 * self.rows - 1 - came) * 2 + 1)
        return there * CORES + core


def normalize(rows, gain):
    rows = rows.astype(jnp.float32)
    center = rows - jnp.mean(rows, axis=-1, keepdims=True)
    spread = jnp.mean(center * center, axis=-1, keepdims=True)
    return center * lax.rsqrt(spread + 1e-06) * gain


def dot(a, b, dims=((1,), (0,))):
    return lax.dot_general(a, b, (dims, ((), ())), preferred_element_type=jnp.float32)


def find_slot(owner, partners, counts, own, listed):
    image = jnp.int32(0)
    index = jnp.int32(0)
    live = jnp.int32(0)
    for a in range(own):
        for k in range(listed):
            partner = partners[a, k]
            hit = jnp.logical_and(k < counts[a], partner // own == owner)
            image = jnp.where(hit, a, image)
            index = jnp.where(hit, lax.rem(partner, own), index)
            live = jnp.where(hit, 1, live)
    return image, index, live


def attend(memory, find_slots, gain, w_kv, spread_q, total, tok):
    width = memory.shape[-1]
    normed = normalize(memory, gain).astype(jnp.bfloat16)
    both = dot(normed, w_kv[...]).astype(jnp.bfloat16)
    for at, (image, live) in enumerate(find_slots()):
        here = slice(at * tok, (at + 1) * tok)
        for g in range(HEADS // 2):
            feats = slice(g * PAIRED, (g + 1) * PAIRED)
            scores = dot(both[here, feats], spread_q[image, feats, :])
            weights = jnp.exp(scores - jnp.max(scores, axis=0, keepdims=True))
            share = live.astype(jnp.float32) / jnp.sum(weights, axis=0, keepdims=True)
            weights = weights.astype(jnp.bfloat16)
            values = both[here, width + g * PAIRED : width + (g + 1) * PAIRED]
            crossed = dot(values, weights, ((0,), (0,)))
            first = crossed[:HEAD_DIM, :tok] * share[:, :tok]
            second = crossed[HEAD_DIM:, tok:] * share[:, tok:]
            total[image, feats, :] += jnp.concatenate([first, second], axis=0)


def first_kernel(ring, slots, own, listed, tok, *refs):
    (tokens, partners, counts, gain_query, gain_memory, w_query, w_key, w_value, w_out) = refs[:9]
    total, spread_q, w_kv, w_out_here, tokens_here, gain_here, picks, table = refs[9:17]
    partners_here, counts_here, gain_query_here, w_query_here, sems = refs[17:]
    width = tokens.shape[-1]
    copies = [
        pltpu.make_async_copy(source, target, sems.at[i])
        for i, (source, target) in enumerate(
            (
                (partners, partners_here),
                (counts, counts_here),
                (tokens, tokens_here),
                (gain_query, gain_query_here),
                (w_query, w_query_here),
                (gain_memory, gain_here),
                (w_key, w_kv.at[:, pl.ds(0, width)]),
                (w_value, w_kv.at[:, pl.ds(width, width)]),
                (w_out, w_out_here),
            )
        )
    ]
    for copy in copies:
        copy.start()
    total[...] = jnp.zeros_like(total)
    for copy in copies[:2]:
        copy.wait()
    for owner in range(ring.chips * CORES):
        image, index, live = find_slot(owner, partners_here, counts_here, own, listed)
        table[0, owner] = image
        table[1, owner] = live
        picks[owner : owner + 1, :] = jnp.full((1, LANES), index.astype(jnp.float32))
    for copy in copies[2:5]:
        copy.wait()
    rows = tokens_here[...].reshape(own * tok, -1)
    normed_query = normalize(rows, gain_query_here[...][None, :]).astype(jnp.bfloat16)
    queries = dot(normed_query, w_query_here[...]).astype(jnp.bfloat16).astype(jnp.float32)
    queries_t = (queries * (1.0 / HEAD_DIM**0.5)).T.astype(jnp.bfloat16)
    zero = jnp.zeros((HEAD_DIM, tok), jnp.bfloat16)
    for a in range(own):
        for h in range(HEADS):
            part = queries_t[h * HEAD_DIM : (h + 1) * HEAD_DIM, a * tok : (a + 1) * tok]
            pieces = [part, zero] if h % 2 == 0 else [zero, part]
            spread_q[a, h * HEAD_DIM : (h + 1) * HEAD_DIM, :] = jnp.concatenate(pieces, axis=1)
    for copy in copies[5:8]:
        copy.wait()
    me = lax.axis_index("img")
    chosen, asked = [], []
    for shift, flip, _ in slots:
        owner = ring.owner(me, shift, flip)
        chosen.append(choose([tokens_here[j] for j in range(own)], picks[pl.ds(owner, 1), :]))
        asked.append((table[0, owner], table[1, owner]))
    attend(jnp.concatenate(chosen, axis=0), lambda: asked, gain_here[...][None, :], w_kv, spread_q, total, tok)
    copies[8].wait()


def choose(images, pick):
    pick = jnp.concatenate([pick] * (images[0].shape[-1] // LANES), axis=1)
    chosen = images[0].astype(jnp.float32)
    for j in range(1, len(images)):
        chosen = jnp.where(pick == j, images[j].astype(jnp.float32), chosen)
    return chosen


def later_kernel(ring, slots, last, own, tok, *refs):
    refs = list(refs)
    take = lambda n: [refs.pop(0) for _ in range(n)]
    sources = [take(n) for _, _, n in slots]
    (arrived,) = take(1) if any(n == 0 for _, _, n in slots) else (None,)
    spread_q, w_kv, gain, picks, table, _ = take(6)
    if last:
        w_out, tokens, counts, total, mixed, mixed_here, counts_here, table_here, sems = refs
    else:
        total, table_here, sems = refs
    copies = [pltpu.make_async_copy(table, table_here, sems.at[0])]
    if last:
        copies.append(pltpu.make_async_copy(counts, counts_here, sems.at[1]))
    for copy in copies:
        copy.start()
    me = lax.axis_index("img")
    owners = [ring.owner(me, shift, flip) for shift, flip, _ in slots]
    chosen = []
    came = 0
    other = 1 - lax.rem(me, CORES)
    for (_, flip, _), arrays, owner in zip(slots, sources, owners):
        if len(arrays) == 1 and len(arrays[0].shape) == 2:
            chosen.append(arrays[0][...].astype(jnp.float32))
            continue
        if not arrays:
            chosen.append(arrived[came].astype(jnp.float32))
            came += 1
            continue
        images = [arrays[0][j] for j in range(own)] if len(arrays) == 1 else [image[:tok, :] for image in arrays]
        chosen.append(choose(images, picks[pl.ds(owner, 1), :]))

    def find_slots():
        for copy in copies:
            copy.wait()
        return [(table_here[0, owner], table_here[1, owner]) for owner in owners]

    attend(jnp.concatenate(chosen, axis=0), find_slots, gain[...][None, :], w_kv, spread_q, total, tok)
    if last:
        context = jnp.concatenate([total[a] / counts_here[a].astype(jnp.float32) for a in range(own)], axis=1)
        context = context.astype(jnp.bfloat16)
        half = tokens.shape[-1] // 2
        copies = []
        for i in range(2):
            part = pl.ds(i * half, half)
            out = dot(context, w_out[:, part], ((0,), (0,)))
            mixed_here[:, :, part] = (tokens[:, :, part].astype(jnp.float32) + out.reshape(own, tok, half)).astype(jnp.bfloat16)
            copies.append(pltpu.make_async_copy(mixed_here.at[:, :, part], mixed.at[:, :, part], sems.at[i]))
            copies[-1].start()
        for copy in copies:
            copy.wait()


HBM = pl.BlockSpec(memory_space=pltpu.HBM)
ANY = pl.BlockSpec(memory_space=pl.ANY)
SMEM = pl.BlockSpec(memory_space=pltpu.SMEM)
VMEM = pl.BlockSpec(memory_space=pltpu.VMEM)


def cost(rows, tok, width):
    return pl.CostEstimate(
        flops=rows * width,
        bytes_accessed=rows * width,
        transcendentals=rows,
    )


def first_stage(ring, slots, operands, own, listed, tok, width):
    devices = ring.chips * CORES
    shapes = [
        jax.ShapeDtypeStruct((own, width, tok), jnp.float32),
        jax.ShapeDtypeStruct((own, width, 2 * tok), jnp.bfloat16),
        jax.ShapeDtypeStruct((width, 2 * width), jnp.bfloat16),
        jax.ShapeDtypeStruct((width, width), jnp.bfloat16),
        jax.ShapeDtypeStruct((own, tok, width), jnp.bfloat16),
        jax.ShapeDtypeStruct((width,), jnp.float32),
        jax.ShapeDtypeStruct((devices, LANES), jnp.float32),
        jax.ShapeDtypeStruct((2, devices), jnp.int32),
    ]
    return pl.pallas_call(
        functools.partial(first_kernel, ring, slots, own, listed, tok),
        out_shape=shapes,
        in_specs=[HBM] * len(operands),
        out_specs=[VMEM] * 7 + [SMEM],
        scratch_shapes=[
            pltpu.SMEM((own, listed), jnp.int32),
            pltpu.SMEM((own,), jnp.int32),
            pltpu.VMEM((width,), jnp.float32),
            pltpu.VMEM((width, width), jnp.bfloat16),
            pltpu.SemaphoreType.DMA((9,)),
        ],
        compiler_params=pltpu.CompilerParams(vmem_limit_bytes=32 << 20),
        cost_estimate=cost(own * tok, tok, width),
    )(*operands)


def later_stage(ring, work, arrived, state, extra, total, own, tok, width):
    slots, sources = zip(*work)
    last = len(extra) > 0
    images = [array for arrays in sources for array in arrays]
    images += [] if arrived is None else [arrived]
    shapes = [jax.ShapeDtypeStruct(total.shape, total.dtype)]
    scratch = [pltpu.SMEM((2, ring.chips * CORES), jnp.int32), pltpu.SemaphoreType.DMA((2,))]
    if last:
        shapes.append(jax.ShapeDtypeStruct((own, tok, width), jnp.bfloat16))
        scratch = [pltpu.VMEM((own, tok, width), jnp.bfloat16), pltpu.SMEM((own,), jnp.int32)] + scratch
    return pl.pallas_call(
        functools.partial(later_kernel, ring, slots, last, own, tok),
        out_shape=shapes,
        in_specs=[VMEM] * (len(images) + 4) + [ANY, VMEM] + ([VMEM, VMEM, ANY] if last else []),
        out_specs=[VMEM] + ([HBM] if last else []),
        scratch_shapes=scratch,
        input_output_aliases={len(images) + 5: 0},
        compiler_params=pltpu.CompilerParams(vmem_limit_bytes=32 << 20),
        cost_estimate=cost(len(slots) * tok, tok, width),
    )(*images, *state, total, *extra)


def pass_kernel(ring, shifts, own, split, *refs):
    each = 1 if split else own
    arrays, refs = refs[: each * len(shifts)], refs[each * len(shifts) :]
    sibling_picks, passed = refs[0], refs[1 + split]
    me = lax.axis_index("img")
    tok = passed.shape[1]
    for i, shift in enumerate(shifts):
        if split:
            images = [arrays[i][j] for j in range(own)]
        else:
            images = [image[:tok, :] for image in arrays[i * own : (i + 1) * own]]
        owner = ring.owner(me, shift, False)
        passed[i] = choose(images, sibling_picks[pl.ds(owner, 1), :]).astype(passed.dtype)
    if split:
        picks, singles = refs[1], refs[3:]
        for i, single in enumerate(singles):
            single[:tok, :] = arrays[i // own][i % own]
        carried = singles[-1]
        carried[tok:, :] = jnp.zeros_like(carried[tok:, :])
        carried[tok:, :LANES] = picks[...].astype(carried.dtype)
        carried[tok:, LANES : 2 * LANES] = sibling_picks[...].astype(carried.dtype)


def pass_stage(ring, work, sibling_picks, split, own, tok, width):
    shifts, arrays = zip(*work)
    arrays = [array for some in arrays for array in some]
    shapes = [jax.ShapeDtypeStruct((len(work), tok, width), jnp.bfloat16)]
    if split:
        shapes += [jax.ShapeDtypeStruct((tok, width), jnp.bfloat16)] * (own * len(work) - 1)
        shapes.append(jax.ShapeDtypeStruct((tok + ring.chips * CORES, width), jnp.bfloat16))
    return pl.pallas_call(
        functools.partial(pass_kernel, ring, shifts, own, len(split)),
        out_shape=shapes,
        in_specs=[VMEM] * (len(arrays) + 1 + len(split)),
        out_specs=[VMEM] * len(shapes),
        compiler_params=pltpu.CompilerParams(vmem_limit_bytes=32 << 20),
        cost_estimate=pl.CostEstimate(flops=len(arrays) * tok * width, bytes_accessed=tok * width, transcendentals=0),
    )(*arrays, sibling_picks, *split)


def far_kernel(ring, shift, own, *refs):
    arrays, carried, outs = refs[:own], refs[own], refs[own + 1 :]
    tok = outs[0].shape[0]
    owner = ring.owner(lax.axis_index("img"), shift, False)
    rows = carried[tok:, : 2 * LANES].astype(jnp.float32)
    rows = jnp.where(lax.broadcasted_iota(jnp.int32, rows.shape, 0) == owner, rows, 0.0)
    pick = jnp.sum(rows, axis=0, keepdims=True)
    for i, out in enumerate(outs):
        images = [image[:tok, :] for image in arrays]
        out[...] = choose(images, pick[:, i * LANES : (i + 1) * LANES]).astype(out.dtype)


def far_stage(ring, shift, images, carried, own, tok, width):
    return pl.pallas_call(
        functools.partial(far_kernel, ring, shift, own),
        out_shape=[jax.ShapeDtypeStruct((tok, width), jnp.bfloat16)] * CORES,
        in_specs=[VMEM] * (own + 1),
        out_specs=[VMEM] * CORES,
        compiler_params=pltpu.CompilerParams(vmem_limit_bytes=32 << 20),
        cost_estimate=pl.CostEstimate(flops=own * tok * width, bytes_accessed=tok * width, transcendentals=0),
    )(*images, carried)


def shards(columns, tokens, partners, counts, gain_query, gain_memory, w_query, w_key, w_value, w_out):
    own, tok, width = tokens.shape
    listed = partners.shape[1]
    ring = Ring(lax.axis_size("img"), columns)
    ahead, back, sibling = ring.onward(1), ring.onward(-1), ring.sibling()
    sizes = dict(own=own, tok=tok, width=width)
    send = lambda array, to: lax.ppermute(array, "img", to)

    far = ring.chips // 2
    assert ring.chips == 2 * far and far > 2 and own == 2
    up, down, theirs = [send(tokens, ahead)], [send(tokens, back)], send(tokens, sibling)
    operands = (tokens, partners, counts, gain_query, gain_memory, w_query, w_key, w_value, w_out)
    operands = [pltpu.with_memory_space_constraint(array, pltpu.HBM) for array in operands]
    total, spread_q, w_kv, w_out_here, tokens_here, gain_here, picks, table = first_stage(
        ring, ((0, False, 1),), operands, listed=listed, **sizes
    )
    cross = [(source, target ^ 1) for source, target in ahead]
    sibling_picks = send(picks, sibling)
    state = (spread_q, w_kv, gain_here, picks, table)
    arrived, behind = None, [((0, True, 1), [theirs])]
    for step in range(1, far):
        down[0], total = lax.optimization_barrier((down[0], total))
        work = [((step, False, len(up)), up), ((-step, False, len(down)), down)] + behind
        passing = [(step, up), (-step, down)]
        if step == 1:
            passed, *singles = pass_stage(ring, passing, sibling_picks, [picks], **sizes)
            up, down = singles[:own], singles[own:]
        else:
            (passed,) = pass_stage(ring, passing, sibling_picks, [], **sizes)
        if step == 2:
            carried = down[1]
        came = send(passed, sibling)
        if step + 1 < far:
            up, down = [send(image, ahead) for image in up], [send(image, back) for image in down]
        else:
            same, other = far_stage(ring, step, up, carried, **sizes)
            same, other = send(same, ahead), send(other, cross)
        (total,) = later_stage(ring, work, arrived, state, (), total, **sizes)
        arrived = came
        behind = [((step, True, 0), []), ((-step, True, 0), [])]
    (total,) = later_stage(ring, behind, arrived, state, (), total, **sizes)
    work = [((far, False, 1), [same]), ((far, True, 1), [other])]
    _, mixed = later_stage(ring, work, None, state, (w_out_here, tokens_here, counts), total, **sizes)
    return mixed


def solution(mesh):
    placed = (
        P(("groups", "img"), None, None),
        P(("groups", "img"), None),
        P(("groups", "img")),
        P(),
        P(),
        P(),
        P(),
        P(),
        P(),
    )
    columns = max(1, 4 // mesh.shape["groups"])
    return jax.shard_map(
        functools.partial(shards, columns),
        mesh=mesh,
        in_specs=placed,
        out_specs=P(("groups", "img"), None, None),
        check_vma=False,
    )
```

```python
import functools

import jax
import jax.numpy as jnp
from jax import lax
from jax.experimental import pallas as pl
from jax.experimental.pallas import tpu as pltpu
from jax.sharding import PartitionSpec as P

HEADS = 12
HEAD_DIM = 64
CORES = 2
LANES = 128
PAIRED = 2 * HEAD_DIM


class Ring:
    def __init__(self, devices, columns):
        self.chips = devices // CORES
        self.columns = columns
        self.rows = self.chips // columns

    def chip(self, place):
        if self.columns == 1:
            return place
        if place < self.rows:
            return place * 2
        return (2 * self.rows - 1 - place) * 2 + 1

    def onward(self, step):
        pairs = []
        for place in range(self.chips):
            for core, way in ((0, step), (1, -step)):
                target = self.chip((place + way) % self.chips)
                pairs.append((self.chip(place) * CORES + core, target * CORES + core))
        return pairs

    def sibling(self):
        return [(i, i ^ 1) for i in range(self.chips * CORES)]

    def pairs(self):
        return [[chip * CORES + core for core in range(CORES)] for chip in range(self.chips)]

    def owner(self, me, shift, flip):
        chip = me // CORES
        core = lax.rem(me, CORES)
        if flip:
            core = 1 - core
        if self.columns == 1:
            place = chip
        else:
            row = chip // 2
            place = jnp.where(lax.rem(chip, 2) == 0, row, 2 * self.rows - 1 - row)
        came = lax.rem(place + self.chips + jnp.where(core == 0, -shift, shift), self.chips)
        if self.columns == 1:
            there = came
        else:
            there = jnp.where(came < self.rows, came * 2, (2 * self.rows - 1 - came) * 2 + 1)
        return there * CORES + core


def normalize(rows, gain):
    rows = rows.astype(jnp.float32)
    center = rows - jnp.mean(rows, axis=-1, keepdims=True)
    spread = jnp.mean(center * center, axis=-1, keepdims=True)
    return center * lax.rsqrt(spread + 1e-06) * gain


def dot(a, b, dims=((1,), (0,))):
    return lax.dot_general(a, b, (dims, ((), ())), preferred_element_type=jnp.float32)


def find_slot(owner, partners, counts, own, listed):
    image = jnp.int32(0)
    index = jnp.int32(0)
    live = jnp.int32(0)
    for a in range(own):
        for k in range(listed):
            partner = partners[a, k]
            hit = jnp.logical_and(k < counts[a], partner // own == owner)
            image = jnp.where(hit, a, image)
            index = jnp.where(hit, lax.rem(partner, own), index)
            live = jnp.where(hit, 1, live)
    return image, index, live


def attend(memory, find_slots, gain, w_kv, spread_q, total, tok):
    width = memory.shape[-1]
    normed = normalize(memory, gain).astype(jnp.bfloat16)
    both = dot(normed, w_kv[...]).astype(jnp.bfloat16)
    for at, (image, live) in enumerate(find_slots()):
        here = slice(at * tok, (at + 1) * tok)
        for g in range(HEADS // 2):
            feats = slice(g * PAIRED, (g + 1) * PAIRED)
            scores = dot(both[here, feats], spread_q[image, feats, :])
            weights = jnp.exp(scores - jnp.max(scores, axis=0, keepdims=True))
            share = live.astype(jnp.float32) / jnp.sum(weights, axis=0, keepdims=True)
            weights = weights.astype(jnp.bfloat16)
            values = both[here, width + g * PAIRED : width + (g + 1) * PAIRED]
            crossed = dot(values, weights, ((0,), (0,)))
            first = crossed[:HEAD_DIM, :tok] * share[:, :tok]
            second = crossed[HEAD_DIM:, tok:] * share[:, tok:]
            total[image, feats, :] += jnp.concatenate([first, second], axis=0)


def first_kernel(ring, slots, own, listed, tok, *refs):
    (tokens, partners, counts, gain_query, gain_memory, w_query, w_key, w_value, w_out) = refs[:9]
    total, spread_q, w_kv, w_out_here, tokens_here, gain_here, picks, table = refs[9:17]
    partners_here, counts_here, gain_query_here, w_query_here, sems = refs[17:]
    width = tokens.shape[-1]
    copies = [
        pltpu.make_async_copy(source, target, sems.at[i])
        for i, (source, target) in enumerate(
            (
                (partners, partners_here),
                (counts, counts_here),
                (tokens, tokens_here),
                (gain_query, gain_query_here),
                (w_query, w_query_here),
                (gain_memory, gain_here),
                (w_key, w_kv.at[:, pl.ds(0, width)]),
                (w_value, w_kv.at[:, pl.ds(width, width)]),
                (w_out, w_out_here),
            )
        )
    ]
    for copy in copies:
        copy.start()
    total[...] = jnp.zeros_like(total)
    for copy in copies[:2]:
        copy.wait()
    for owner in range(ring.chips * CORES):
        image, index, live = find_slot(owner, partners_here, counts_here, own, listed)
        table[0, owner] = image
        table[1, owner] = live
        picks[owner : owner + 1, :] = jnp.full((1, LANES), index.astype(jnp.float32))
    for copy in copies[2:5]:
        copy.wait()
    rows = tokens_here[...].reshape(own * tok, -1)
    normed_query = normalize(rows, gain_query_here[...][None, :]).astype(jnp.bfloat16)
    queries = dot(normed_query, w_query_here[...]).astype(jnp.bfloat16).astype(jnp.float32)
    queries_t = (queries * (1.0 / HEAD_DIM**0.5)).T.astype(jnp.bfloat16)
    zero = jnp.zeros((HEAD_DIM, tok), jnp.bfloat16)
    for a in range(own):
        for h in range(HEADS):
            part = queries_t[h * HEAD_DIM : (h + 1) * HEAD_DIM, a * tok : (a + 1) * tok]
            pieces = [part, zero] if h % 2 == 0 else [zero, part]
            spread_q[a, h * HEAD_DIM : (h + 1) * HEAD_DIM, :] = jnp.concatenate(pieces, axis=1)
    for copy in copies[5:8]:
        copy.wait()
    me = lax.axis_index("img")
    chosen, asked = [], []
    for shift, flip, _ in slots:
        owner = ring.owner(me, shift, flip)
        chosen.append(choose([tokens_here[j] for j in range(own)], picks[pl.ds(owner, 1), :]))
        asked.append((table[0, owner], table[1, owner]))
    attend(jnp.concatenate(chosen, axis=0), lambda: asked, gain_here[...][None, :], w_kv, spread_q, total, tok)
    copies[8].wait()


def choose(images, pick):
    pick = jnp.concatenate([pick] * (images[0].shape[-1] // LANES), axis=1)
    chosen = images[0].astype(jnp.float32)
    for j in range(1, len(images)):
        chosen = jnp.where(pick == j, images[j].astype(jnp.float32), chosen)
    return chosen


def later_kernel(ring, slots, last, own, tok, *refs):
    refs = list(refs)
    take = lambda n: [refs.pop(0) for _ in range(n)]
    sources = [take(n) for _, _, n in slots]
    (arrived,) = take(1) if any(n == 0 for _, _, n in slots) else (None,)
    spread_q, w_kv, gain, picks, table, total_in = take(6)
    if last:
        w_out, tokens, counts, total, mixed, mixed_here, counts_here, table_here, sems = refs
    else:
        total, table_here, sems = refs
    copies = [pltpu.make_async_copy(table, table_here, sems.at[0])]
    if last:
        copies.append(pltpu.make_async_copy(counts, counts_here, sems.at[1]))
    for copy in copies:
        copy.start()
    total[...] = total_in[...]
    me = lax.axis_index("img")
    owners = [ring.owner(me, shift, flip) for shift, flip, _ in slots]
    chosen = []
    came = 0
    other = 1 - lax.rem(me, CORES)
    for (_, flip, _), arrays, owner in zip(slots, sources, owners):
        if len(arrays) == 1 and len(arrays[0].shape) == 2:
            chosen.append(arrays[0][...].astype(jnp.float32))
            continue
        if not arrays:
            chosen.append(arrived[came].astype(jnp.float32))
            came += 1
            continue
        images = [arrays[0][j] for j in range(own)] if len(arrays) == 1 else [image[:tok, :] for image in arrays]
        chosen.append(choose(images, picks[pl.ds(owner, 1), :]))

    def find_slots():
        for copy in copies:
            copy.wait()
        return [(table_here[0, owner], table_here[1, owner]) for owner in owners]

    attend(jnp.concatenate(chosen, axis=0), find_slots, gain[...][None, :], w_kv, spread_q, total, tok)
    if last:
        context = jnp.concatenate([total[a] / counts_here[a].astype(jnp.float32) for a in range(own)], axis=1)
        context = context.astype(jnp.bfloat16)
        half = tokens.shape[-1] // 2
        copies = []
        for i in range(2):
            part = pl.ds(i * half, half)
            out = dot(context, w_out[:, part], ((0,), (0,)))
            mixed_here[:, :, part] = (tokens[:, :, part].astype(jnp.float32) + out.reshape(own, tok, half)).astype(jnp.bfloat16)
            copies.append(pltpu.make_async_copy(mixed_here.at[:, :, part], mixed.at[:, :, part], sems.at[i]))
            copies[-1].start()
        for copy in copies:
            copy.wait()


HBM = pl.BlockSpec(memory_space=pltpu.HBM)
ANY = pl.BlockSpec(memory_space=pl.ANY)
SMEM = pl.BlockSpec(memory_space=pltpu.SMEM)
VMEM = pl.BlockSpec(memory_space=pltpu.VMEM)


def cost(rows, tok, width):
    return pl.CostEstimate(
        flops=rows * width,
        bytes_accessed=rows * width,
        transcendentals=rows,
    )


def first_stage(ring, slots, operands, own, listed, tok, width):
    devices = ring.chips * CORES
    shapes = [
        jax.ShapeDtypeStruct((own, width, tok), jnp.float32),
        jax.ShapeDtypeStruct((own, width, 2 * tok), jnp.bfloat16),
        jax.ShapeDtypeStruct((width, 2 * width), jnp.bfloat16),
        jax.ShapeDtypeStruct((width, width), jnp.bfloat16),
        jax.ShapeDtypeStruct((own, tok, width), jnp.bfloat16),
        jax.ShapeDtypeStruct((width,), jnp.float32),
        jax.ShapeDtypeStruct((devices, LANES), jnp.float32),
        jax.ShapeDtypeStruct((2, devices), jnp.int32),
    ]
    return pl.pallas_call(
        functools.partial(first_kernel, ring, slots, own, listed, tok),
        out_shape=shapes,
        in_specs=[HBM] * len(operands),
        out_specs=[VMEM] * 7 + [SMEM],
        scratch_shapes=[
            pltpu.SMEM((own, listed), jnp.int32),
            pltpu.SMEM((own,), jnp.int32),
            pltpu.VMEM((width,), jnp.float32),
            pltpu.VMEM((width, width), jnp.bfloat16),
            pltpu.SemaphoreType.DMA((9,)),
        ],
        compiler_params=pltpu.CompilerParams(vmem_limit_bytes=32 << 20),
        cost_estimate=cost(own * tok, tok, width),
    )(*operands)


def later_stage(ring, work, arrived, state, extra, total, own, tok, width):
    slots, sources = zip(*work)
    last = len(extra) > 0
    images = [array for arrays in sources for array in arrays]
    images += [] if arrived is None else [arrived]
    shapes = [jax.ShapeDtypeStruct(total.shape, total.dtype)]
    scratch = [pltpu.SMEM((2, ring.chips * CORES), jnp.int32), pltpu.SemaphoreType.DMA((2,))]
    if last:
        shapes.append(jax.ShapeDtypeStruct((own, tok, width), jnp.bfloat16))
        scratch = [pltpu.VMEM((own, tok, width), jnp.bfloat16), pltpu.SMEM((own,), jnp.int32)] + scratch
    return pl.pallas_call(
        functools.partial(later_kernel, ring, slots, last, own, tok),
        out_shape=shapes,
        in_specs=[VMEM] * (len(images) + 4) + [ANY, VMEM] + ([VMEM, VMEM, ANY] if last else []),
        out_specs=[VMEM] + ([HBM] if last else []),
        scratch_shapes=scratch,
        input_output_aliases={len(images) + 5: 0},
        compiler_params=pltpu.CompilerParams(vmem_limit_bytes=32 << 20),
        cost_estimate=cost(len(slots) * tok, tok, width),
    )(*images, *state, total, *extra)


def pass_kernel(ring, shifts, own, split, *refs):
    each = 1 if split else own
    arrays, refs = refs[: each * len(shifts)], refs[each * len(shifts) :]
    sibling_picks, passed = refs[0], refs[1 + split]
    me = lax.axis_index("img")
    tok = passed.shape[1]
    for i, shift in enumerate(shifts):
        if split:
            images = [arrays[i][j] for j in range(own)]
        else:
            images = [image[:tok, :] for image in arrays[i * own : (i + 1) * own]]
        owner = ring.owner(me, shift, False)
        passed[i] = choose(images, sibling_picks[pl.ds(owner, 1), :]).astype(passed.dtype)
    if split:
        picks, singles = refs[1], refs[3:]
        for i, single in enumerate(singles):
            single[:tok, :] = arrays[i // own][i % own]
        carried = singles[-1]
        carried[tok:, :] = jnp.zeros_like(carried[tok:, :])
        carried[tok:, :LANES] = picks[...].astype(carried.dtype)
        carried[tok:, LANES : 2 * LANES] = sibling_picks[...].astype(carried.dtype)


def pass_stage(ring, work, sibling_picks, split, own, tok, width):
    shifts, arrays = zip(*work)
    arrays = [array for some in arrays for array in some]
    shapes = [jax.ShapeDtypeStruct((len(work), tok, width), jnp.bfloat16)]
    if split:
        shapes += [jax.ShapeDtypeStruct((tok, width), jnp.bfloat16)] * (own * len(work) - 1)
        shapes.append(jax.ShapeDtypeStruct((tok + ring.chips * CORES, width), jnp.bfloat16))
    return pl.pallas_call(
        functools.partial(pass_kernel, ring, shifts, own, len(split)),
        out_shape=shapes,
        in_specs=[VMEM] * (len(arrays) + 1 + len(split)),
        out_specs=[VMEM] * len(shapes),
        compiler_params=pltpu.CompilerParams(vmem_limit_bytes=32 << 20),
        cost_estimate=pl.CostEstimate(flops=len(arrays) * tok * width, bytes_accessed=tok * width, transcendentals=0),
    )(*arrays, sibling_picks, *split)


def far_kernel(ring, shift, own, *refs):
    arrays, carried, outs = refs[:own], refs[own], refs[own + 1 :]
    tok = outs[0].shape[0]
    owner = ring.owner(lax.axis_index("img"), shift, False)
    rows = carried[tok:, : 2 * LANES].astype(jnp.float32)
    rows = jnp.where(lax.broadcasted_iota(jnp.int32, rows.shape, 0) == owner, rows, 0.0)
    pick = jnp.sum(rows, axis=0, keepdims=True)
    for i, out in enumerate(outs):
        images = [image[:tok, :] for image in arrays]
        out[...] = choose(images, pick[:, i * LANES : (i + 1) * LANES]).astype(out.dtype)


def far_stage(ring, shift, images, carried, own, tok, width):
    return pl.pallas_call(
        functools.partial(far_kernel, ring, shift, own),
        out_shape=[jax.ShapeDtypeStruct((tok, width), jnp.bfloat16)] * CORES,
        in_specs=[VMEM] * (own + 1),
        out_specs=[VMEM] * CORES,
        compiler_params=pltpu.CompilerParams(vmem_limit_bytes=32 << 20),
        cost_estimate=pl.CostEstimate(flops=own * tok * width, bytes_accessed=tok * width, transcendentals=0),
    )(*images, carried)


def shards(columns, tokens, partners, counts, gain_query, gain_memory, w_query, w_key, w_value, w_out):
    own, tok, width = tokens.shape
    listed = partners.shape[1]
    ring = Ring(lax.axis_size("img"), columns)
    ahead, back, sibling = ring.onward(1), ring.onward(-1), ring.sibling()
    sizes = dict(own=own, tok=tok, width=width)
    send = lambda array, to: lax.ppermute(array, "img", to)

    far = ring.chips // 2
    assert ring.chips == 2 * far and far > 2 and own == 2
    up, down, theirs = [send(tokens, ahead)], [send(tokens, back)], send(tokens, sibling)
    operands = (tokens, partners, counts, gain_query, gain_memory, w_query, w_key, w_value, w_out)
    operands = [pltpu.with_memory_space_constraint(array, pltpu.HBM) for array in operands]
    total, spread_q, w_kv, w_out_here, tokens_here, gain_here, picks, table = first_stage(
        ring, ((0, False, 1),), operands, listed=listed, **sizes
    )
    cross = [(source, target ^ 1) for source, target in ahead]
    sibling_picks = send(picks, sibling)
    state = (spread_q, w_kv, gain_here, picks, table)
    arrived, behind = None, [((0, True, 1), [theirs])]
    for step in range(1, far):
        up[0], down[0], total = lax.optimization_barrier((up[0], down[0], total))
        work = [((step, False, len(up)), up), ((-step, False, len(down)), down)] + behind
        passing = [(step, up), (-step, down)]
        if step == 1:
            passed, *singles = pass_stage(ring, passing, sibling_picks, [picks], **sizes)
            up, down = singles[:own], singles[own:]
        else:
            (passed,) = pass_stage(ring, passing, sibling_picks, [], **sizes)
        if step == 2:
            carried = down[1]
        came = send(passed, sibling)
        if step + 1 < far:
            up, down = [send(image, ahead) for image in up], [send(image, back) for image in down]
        else:
            same, other = far_stage(ring, step, up, carried, **sizes)
            same, other = send(same, ahead), send(other, cross)
        (total,) = later_stage(ring, work, arrived, state, (), total, **sizes)
        arrived = came
        behind = [((step, True, 0), []), ((-step, True, 0), [])]
    (total,) = later_stage(ring, behind, arrived, state, (), total, **sizes)
    work = [((far, False, 1), [same]), ((far, True, 1), [other])]
    _, mixed = later_stage(ring, work, None, state, (w_out_here, tokens_here, counts), total, **sizes)
    return mixed


def solution(mesh):
    placed = (
        P(("groups", "img"), None, None),
        P(("groups", "img"), None),
        P(("groups", "img")),
        P(),
        P(),
        P(),
        P(),
        P(),
        P(),
    )
    columns = max(1, 4 // mesh.shape["groups"])
    return jax.shard_map(
        functools.partial(shards, columns),
        mesh=mesh,
        in_specs=placed,
        out_specs=P(("groups", "img"), None, None),
        check_vma=False,
    )
```

```python
import functools

import jax
import jax.numpy as jnp
from jax import lax
from jax.experimental import pallas as pl
from jax.experimental.pallas import tpu as pltpu
from jax.sharding import PartitionSpec as P

HEADS = 12
HEAD_DIM = 64
CORES = 2
LANES = 128
PAIRED = 2 * HEAD_DIM


class Ring:
    def __init__(self, devices, columns):
        self.chips = devices // CORES
        self.columns = columns
        self.rows = self.chips // columns

    def chip(self, place):
        if self.columns == 1:
            return place
        if place < self.rows:
            return place * 2
        return (2 * self.rows - 1 - place) * 2 + 1

    def onward(self, step):
        pairs = []
        for place in range(self.chips):
            for core, way in ((0, step), (1, -step)):
                target = self.chip((place + way) % self.chips)
                pairs.append((self.chip(place) * CORES + core, target * CORES + core))
        return pairs

    def sibling(self):
        return [(i, i ^ 1) for i in range(self.chips * CORES)]

    def pairs(self):
        return [[chip * CORES + core for core in range(CORES)] for chip in range(self.chips)]

    def owner(self, me, shift, flip):
        chip = me // CORES
        core = lax.rem(me, CORES)
        if flip:
            core = 1 - core
        if self.columns == 1:
            place = chip
        else:
            row = chip // 2
            place = jnp.where(lax.rem(chip, 2) == 0, row, 2 * self.rows - 1 - row)
        came = lax.rem(place + self.chips + jnp.where(core == 0, -shift, shift), self.chips)
        if self.columns == 1:
            there = came
        else:
            there = jnp.where(came < self.rows, came * 2, (2 * self.rows - 1 - came) * 2 + 1)
        return there * CORES + core


def normalize(rows, gain):
    rows = rows.astype(jnp.float32)
    center = rows - jnp.mean(rows, axis=-1, keepdims=True)
    spread = jnp.mean(center * center, axis=-1, keepdims=True)
    return center * lax.rsqrt(spread + 1e-06) * gain


def dot(a, b, dims=((1,), (0,))):
    return lax.dot_general(a, b, (dims, ((), ())), preferred_element_type=jnp.float32)


def find_slot(owner, partners, counts, own, listed):
    image = jnp.int32(0)
    index = jnp.int32(0)
    live = jnp.int32(0)
    for a in range(own):
        for k in range(listed):
            partner = partners[a, k]
            hit = jnp.logical_and(k < counts[a], partner // own == owner)
            image = jnp.where(hit, a, image)
            index = jnp.where(hit, lax.rem(partner, own), index)
            live = jnp.where(hit, 1, live)
    return image, index, live


def attend(memory, find_slots, gain, w_kv, spread_q, total, tok):
    width = memory.shape[-1]
    normed = normalize(memory, gain).astype(jnp.bfloat16)
    both = dot(normed, w_kv[...]).astype(jnp.bfloat16)
    for at, (image, live) in enumerate(find_slots()):
        here = slice(at * tok, (at + 1) * tok)
        for g in range(HEADS // 2):
            feats = slice(g * PAIRED, (g + 1) * PAIRED)
            scores = dot(both[here, feats], spread_q[image, feats, :])
            weights = jnp.exp(scores - jnp.max(scores, axis=0, keepdims=True))
            share = live.astype(jnp.float32) / jnp.sum(weights, axis=0, keepdims=True)
            weights = weights.astype(jnp.bfloat16)
            values = both[here, width + g * PAIRED : width + (g + 1) * PAIRED]
            crossed = dot(values, weights, ((0,), (0,)))
            first = crossed[:HEAD_DIM, :tok] * share[:, :tok]
            second = crossed[HEAD_DIM:, tok:] * share[:, tok:]
            total[image, feats, :] += jnp.concatenate([first, second], axis=0)


def first_kernel(ring, slots, own, listed, tok, *refs):
    (tokens, partners, counts, gain_query, gain_memory, w_query, w_key, w_value, w_out) = refs[:9]
    total, spread_q, w_kv, w_out_here, tokens_here, gain_here, picks, table = refs[9:17]
    partners_here, counts_here, gain_query_here, w_query_here, sems = refs[17:]
    width = tokens.shape[-1]
    copies = [
        pltpu.make_async_copy(source, target, sems.at[i])
        for i, (source, target) in enumerate(
            (
                (partners, partners_here),
                (counts, counts_here),
                (tokens, tokens_here),
                (gain_query, gain_query_here),
                (w_query, w_query_here),
                (gain_memory, gain_here),
                (w_key, w_kv.at[:, pl.ds(0, width)]),
                (w_value, w_kv.at[:, pl.ds(width, width)]),
                (w_out, w_out_here),
            )
        )
    ]
    for copy in copies:
        copy.start()
    total[...] = jnp.zeros_like(total)
    for copy in copies[:2]:
        copy.wait()
    for owner in range(ring.chips * CORES):
        image, index, live = find_slot(owner, partners_here, counts_here, own, listed)
        table[0, owner] = image
        table[1, owner] = live
        picks[owner : owner + 1, :] = jnp.full((1, LANES), index.astype(jnp.float32))
    for copy in copies[2:5]:
        copy.wait()
    rows = tokens_here[...].reshape(own * tok, -1)
    normed_query = normalize(rows, gain_query_here[...][None, :]).astype(jnp.bfloat16)
    queries = dot(normed_query, w_query_here[...]).astype(jnp.bfloat16).astype(jnp.float32)
    queries_t = (queries * (1.0 / HEAD_DIM**0.5)).T.astype(jnp.bfloat16)
    zero = jnp.zeros((HEAD_DIM, tok), jnp.bfloat16)
    for a in range(own):
        for h in range(HEADS):
            part = queries_t[h * HEAD_DIM : (h + 1) * HEAD_DIM, a * tok : (a + 1) * tok]
            pieces = [part, zero] if h % 2 == 0 else [zero, part]
            spread_q[a, h * HEAD_DIM : (h + 1) * HEAD_DIM, :] = jnp.concatenate(pieces, axis=1)
    for copy in copies[5:8]:
        copy.wait()
    me = lax.axis_index("img")
    chosen, asked = [], []
    for shift, flip, _ in slots:
        owner = ring.owner(me, shift, flip)
        chosen.append(choose([tokens_here[j] for j in range(own)], picks[pl.ds(owner, 1), :]))
        asked.append((table[0, owner], table[1, owner]))
    attend(jnp.concatenate(chosen, axis=0), lambda: asked, gain_here[...][None, :], w_kv, spread_q, total, tok)
    copies[8].wait()


def choose(images, pick):
    pick = jnp.concatenate([pick] * (images[0].shape[-1] // LANES), axis=1)
    chosen = images[0].astype(jnp.float32)
    for j in range(1, len(images)):
        chosen = jnp.where(pick == j, images[j].astype(jnp.float32), chosen)
    return chosen


def later_kernel(ring, slots, last, own, tok, *refs):
    refs = list(refs)
    take = lambda n: [refs.pop(0) for _ in range(n)]
    sources = [take(n) for _, _, n in slots]
    (arrived,) = take(1) if any(n == 0 for _, _, n in slots) else (None,)
    spread_q, w_kv, gain, picks, table, total_in = take(6)
    if last:
        w_out, tokens, counts, total, mixed, mixed_here, counts_here, table_here, sems = refs
    else:
        total, table_here, sems = refs
    copies = [pltpu.make_async_copy(table, table_here, sems.at[0])]
    if last:
        copies.append(pltpu.make_async_copy(counts, counts_here, sems.at[1]))
    for copy in copies:
        copy.start()
    total[...] = total_in[...]
    me = lax.axis_index("img")
    owners = [ring.owner(me, shift, flip) for shift, flip, _ in slots]
    chosen = []
    came = 0
    other = 1 - lax.rem(me, CORES)
    for (_, flip, _), arrays, owner in zip(slots, sources, owners):
        if len(arrays) == 1 and len(arrays[0].shape) == 2:
            chosen.append(arrays[0][...].astype(jnp.float32))
            continue
        if not arrays:
            chosen.append(arrived[came].astype(jnp.float32))
            came += 1
            continue
        images = [arrays[0][j] for j in range(own)] if len(arrays) == 1 else [image[:tok, :] for image in arrays]
        chosen.append(choose(images, picks[pl.ds(owner, 1), :]))

    def find_slots():
        for copy in copies:
            copy.wait()
        return [(table_here[0, owner], table_here[1, owner]) for owner in owners]

    attend(jnp.concatenate(chosen, axis=0), find_slots, gain[...][None, :], w_kv, spread_q, total, tok)
    if last:
        context = jnp.concatenate([total[a] / counts_here[a].astype(jnp.float32) for a in range(own)], axis=1)
        context = context.astype(jnp.bfloat16)
        half = tokens.shape[-1] // 2
        copies = []
        for i in range(2):
            part = pl.ds(i * half, half)
            out = dot(context, w_out[:, part], ((0,), (0,)))
            mixed_here[:, :, part] = (tokens[:, :, part].astype(jnp.float32) + out.reshape(own, tok, half)).astype(jnp.bfloat16)
            copies.append(pltpu.make_async_copy(mixed_here.at[:, :, part], mixed.at[:, :, part], sems.at[i]))
            copies[-1].start()
        for copy in copies:
            copy.wait()


HBM = pl.BlockSpec(memory_space=pltpu.HBM)
ANY = pl.BlockSpec(memory_space=pl.ANY)
SMEM = pl.BlockSpec(memory_space=pltpu.SMEM)
VMEM = pl.BlockSpec(memory_space=pltpu.VMEM)


def cost(rows, tok, width):
    return pl.CostEstimate(
        flops=rows * width,
        bytes_accessed=rows * width,
        transcendentals=rows,
    )


def first_stage(ring, slots, operands, own, listed, tok, width):
    devices = ring.chips * CORES
    shapes = [
        jax.ShapeDtypeStruct((own, width, tok), jnp.float32),
        jax.ShapeDtypeStruct((own, width, 2 * tok), jnp.bfloat16),
        jax.ShapeDtypeStruct((width, 2 * width), jnp.bfloat16),
        jax.ShapeDtypeStruct((width, width), jnp.bfloat16),
        jax.ShapeDtypeStruct((own, tok, width), jnp.bfloat16),
        jax.ShapeDtypeStruct((width,), jnp.float32),
        jax.ShapeDtypeStruct((devices, LANES), jnp.float32),
        jax.ShapeDtypeStruct((2, devices), jnp.int32),
    ]
    return pl.pallas_call(
        functools.partial(first_kernel, ring, slots, own, listed, tok),
        out_shape=shapes,
        in_specs=[HBM] * len(operands),
        out_specs=[VMEM] * 7 + [SMEM],
        scratch_shapes=[
            pltpu.SMEM((own, listed), jnp.int32),
            pltpu.SMEM((own,), jnp.int32),
            pltpu.VMEM((width,), jnp.float32),
            pltpu.VMEM((width, width), jnp.bfloat16),
            pltpu.SemaphoreType.DMA((9,)),
        ],
        compiler_params=pltpu.CompilerParams(vmem_limit_bytes=32 << 20),
        cost_estimate=cost(own * tok, tok, width),
    )(*operands)


def later_stage(ring, work, arrived, state, extra, total, own, tok, width):
    slots, sources = zip(*work)
    last = len(extra) > 0
    images = [array for arrays in sources for array in arrays]
    images += [] if arrived is None else [arrived]
    shapes = [jax.ShapeDtypeStruct(total.shape, total.dtype)]
    scratch = [pltpu.SMEM((2, ring.chips * CORES), jnp.int32), pltpu.SemaphoreType.DMA((2,))]
    if last:
        shapes.append(jax.ShapeDtypeStruct((own, tok, width), jnp.bfloat16))
        scratch = [pltpu.VMEM((own, tok, width), jnp.bfloat16), pltpu.SMEM((own,), jnp.int32)] + scratch
    return pl.pallas_call(
        functools.partial(later_kernel, ring, slots, last, own, tok),
        out_shape=shapes,
        in_specs=[VMEM] * (len(images) + 4) + [ANY, VMEM] + ([VMEM, VMEM, ANY] if last else []),
        out_specs=[VMEM] + ([HBM] if last else []),
        scratch_shapes=scratch,
        input_output_aliases={len(images) + 5: 0},
        compiler_params=pltpu.CompilerParams(vmem_limit_bytes=32 << 20),
        cost_estimate=cost(len(slots) * tok, tok, width),
    )(*images, *state, total, *extra)


def pass_kernel(ring, shifts, own, split, *refs):
    each = 1 if split else own
    arrays, refs = refs[: each * len(shifts)], refs[each * len(shifts) :]
    sibling_picks, passed = refs[0], refs[1 + split]
    me = lax.axis_index("img")
    tok = passed.shape[1]
    for i, shift in enumerate(shifts):
        if split:
            images = [arrays[i][j] for j in range(own)]
        else:
            images = [image[:tok, :] for image in arrays[i * own : (i + 1) * own]]
        owner = ring.owner(me, shift, False)
        passed[i] = choose(images, sibling_picks[pl.ds(owner, 1), :]).astype(passed.dtype)
    if split:
        picks, singles = refs[1], refs[3:]
        for i, single in enumerate(singles):
            single[:tok, :] = arrays[i // own][i % own]
        carried = singles[-1]
        carried[tok:, :] = jnp.zeros_like(carried[tok:, :])
        carried[tok:, :LANES] = picks[...].astype(carried.dtype)
        carried[tok:, LANES : 2 * LANES] = sibling_picks[...].astype(carried.dtype)


def pass_stage(ring, work, sibling_picks, split, own, tok, width):
    shifts, arrays = zip(*work)
    arrays = [array for some in arrays for array in some]
    shapes = [jax.ShapeDtypeStruct((len(work), tok, width), jnp.bfloat16)]
    if split:
        shapes += [jax.ShapeDtypeStruct((tok, width), jnp.bfloat16)] * (own * len(work) - 1)
        shapes.append(jax.ShapeDtypeStruct((tok + ring.chips * CORES, width), jnp.bfloat16))
    return pl.pallas_call(
        functools.partial(pass_kernel, ring, shifts, own, len(split)),
        out_shape=shapes,
        in_specs=[VMEM] * (len(arrays) + 1 + len(split)),
        out_specs=[VMEM] * len(shapes),
        compiler_params=pltpu.CompilerParams(vmem_limit_bytes=32 << 20),
        cost_estimate=pl.CostEstimate(flops=len(arrays) * tok * width, bytes_accessed=tok * width, transcendentals=0),
    )(*arrays, sibling_picks, *split)


def far_kernel(ring, shift, own, *refs):
    arrays, carried, outs = refs[:own], refs[own], refs[own + 1 :]
    tok = outs[0].shape[0]
    owner = ring.owner(lax.axis_index("img"), shift, False)
    rows = carried[tok:, : 2 * LANES].astype(jnp.float32)
    rows = jnp.where(lax.broadcasted_iota(jnp.int32, rows.shape, 0) == owner, rows, 0.0)
    pick = jnp.sum(rows, axis=0, keepdims=True)
    for i, out in enumerate(outs):
        images = [image[:tok, :] for image in arrays]
        out[...] = choose(images, pick[:, i * LANES : (i + 1) * LANES]).astype(out.dtype)


def far_stage(ring, shift, images, carried, own, tok, width):
    return pl.pallas_call(
        functools.partial(far_kernel, ring, shift, own),
        out_shape=[jax.ShapeDtypeStruct((tok, width), jnp.bfloat16)] * CORES,
        in_specs=[VMEM] * (own + 1),
        out_specs=[VMEM] * CORES,
        compiler_params=pltpu.CompilerParams(vmem_limit_bytes=32 << 20),
        cost_estimate=pl.CostEstimate(flops=own * tok * width, bytes_accessed=tok * width, transcendentals=0),
    )(*images, carried)


def shards(columns, tokens, partners, counts, gain_query, gain_memory, w_query, w_key, w_value, w_out):
    own, tok, width = tokens.shape
    listed = partners.shape[1]
    ring = Ring(lax.axis_size("img"), columns)
    ahead, back, sibling = ring.onward(1), ring.onward(-1), ring.sibling()
    sizes = dict(own=own, tok=tok, width=width)
    send = lambda array, to: lax.ppermute(array, "img", to)

    far = ring.chips // 2
    assert ring.chips == 2 * far and far > 2 and own == 2
    up, down, theirs = [send(tokens, ahead)], [send(tokens, back)], send(tokens, sibling)
    operands = (tokens, partners, counts, gain_query, gain_memory, w_query, w_key, w_value, w_out)
    operands = [pltpu.with_memory_space_constraint(array, pltpu.HBM) for array in operands]
    total, spread_q, w_kv, w_out_here, tokens_here, gain_here, picks, table = first_stage(
        ring, ((0, False, 1),), operands, listed=listed, **sizes
    )
    cross = [(source, target ^ 1) for source, target in ahead]
    sibling_picks = send(picks, sibling)
    state = (spread_q, w_kv, gain_here, picks, table)
    arrived, behind = None, [((0, True, 1), [theirs])]
    for step in range(1, far):
        up[0], down[0], total = lax.optimization_barrier((up[0], down[0], total))
        work = [((step, False, len(up)), up), ((-step, False, len(down)), down)] + behind
        if step + 1 == far:
            same, other = far_stage(ring, step, up, carried, **sizes)
            same, other, up, down = lax.optimization_barrier((same, other, up, down))
            same, other = send(same, ahead), send(other, cross)
        passing = [(step, up), (-step, down)]
        if step == 1:
            passed, *singles = pass_stage(ring, passing, sibling_picks, [picks], **sizes)
            up, down = singles[:own], singles[own:]
        else:
            (passed,) = pass_stage(ring, passing, sibling_picks, [], **sizes)
        if step == 2:
            carried = down[1]
        came = send(passed, sibling)
        if step + 1 < far:
            up, down = [send(image, ahead) for image in up], [send(image, back) for image in down]
        (total,) = later_stage(ring, work, arrived, state, (), total, **sizes)
        arrived = came
        behind = [((step, True, 0), []), ((-step, True, 0), [])]
    (total,) = later_stage(ring, behind, arrived, state, (), total, **sizes)
    work = [((far, False, 1), [same]), ((far, True, 1), [other])]
    _, mixed = later_stage(ring, work, None, state, (w_out_here, tokens_here, counts), total, **sizes)
    return mixed


def solution(mesh):
    placed = (
        P(("groups", "img"), None, None),
        P(("groups", "img"), None),
        P(("groups", "img")),
        P(),
        P(),
        P(),
        P(),
        P(),
        P(),
    )
    columns = max(1, 4 // mesh.shape["groups"])
    return jax.shard_map(
        functools.partial(shards, columns),
        mesh=mesh,
        in_specs=placed,
        out_specs=P(("groups", "img"), None, None),
        check_vma=False,
    )
```
